256 devices in a mesh: row: 8 (over x, y_hi), col: 4 (over y_lo, core), depth: 8 (over z).
Axes of the slice: x: 4, y: 4 (y_hi: 2, y_lo: 2; y = y_hi * 2 + y_lo), z: 8, core: 2. Of those that a mesh axis runs over, the one named last changes fastest.
Arguments:
- cotangent: bfloat16 [2048, 24576], P(('depth', 'row'), 'col'), may hold values from -8 to 8
- activations: bfloat16 [2048, 6144], P('depth', ('row', 'col')), may hold values from -8 to 8
- weight: bfloat16 [24576, 6144], P(('col', 'depth'), 'row'), may hold values from -0.0390625 to 0.0390625
- row_prev: float32 [24576], P(('col', 'depth')), as said below
- col_prev: float32 [6144], P('row'), as said below
Outputs:
- input_grad: bfloat16 [2048, 6144], P('depth', ('row', 'col'))
- update: float32 [24576, 6144], P(('col', 'depth'), 'row')
The draws below stay inside these ranges and needn't reach their ends.
Inputs may be any that keep to these rules, and one draw needn't show every extreme that they name: `row_prev`: positive. `col_prev`: positive.
All inputs are finite; a program needn't handle non-finite values.
Results may differ from the reference program's by a relative error of at most 0.001.
Values may be sent and summed in bfloat16 or wider, within the bound.
No kernel may reach another device: no remote copies, remote signals or barrier semaphores. Data moves between devices by JAX's collectives and lax.ppermute only.
A program may use at most 128 MiB of HBM per device.

```python
import jax
import jax.numpy as jnp
from jax import lax

D = 6144
FF = 24576
BLOCK = 256
TOKENS = 2048


def column_factor(key, width, lowest, highest):
    spread_part = jnp.exp(jax.random.uniform(key, (width,), jnp.float32, jnp.log(lowest), jnp.log(highest)))
    slope = 1.0 + 2.0 * jnp.arange(width, dtype=jnp.float32) / width
    return spread_part * slope / 3.0


def draw_cotangent(key, part):
    key = jax.random.fold_in(key, 11)
    factor_key, value_key = jax.random.split(key, 2)
    factor = column_factor(factor_key, FF, 0.3, 3.0)
    values = jax.random.normal(value_key, (TOKENS, FF), jnp.float32)
    return jnp.clip(values * factor[None, :], -8.0, 8.0).astype(jnp.bfloat16)


def draw_activations(key, part):
    key = jax.random.fold_in(key, 12)
    factor_key, value_key = jax.random.split(key, 2)
    factor = column_factor(factor_key, D, 0.3, 3.0)
    values = jax.random.normal(value_key, (TOKENS, D), jnp.float32)
    return jnp.clip(values * factor[None, :], -8.0, 8.0).astype(jnp.bfloat16)


def draw_row_prev(key, part):
    key = jax.random.fold_in(key, 13)
    falling = 1.0 - 2.0 / 3.0 * jnp.arange(FF, dtype=jnp.float32) / FF
    levels = jnp.exp(jax.random.uniform(key, (FF,), jnp.float32, jnp.log(0.01), jnp.log(0.2)))
    return (TOKENS * levels * falling).astype(jnp.float32)


def draw_col_prev(key, part):
    key = jax.random.fold_in(key, 14)
    falling = 1.0 - 2.0 / 3.0 * jnp.arange(D, dtype=jnp.float32) / D
    levels = jnp.exp(jax.random.uniform(key, (D,), jnp.float32, jnp.log(0.01), jnp.log(0.2)))
    return (TOKENS * levels * falling).astype(jnp.float32)


def shard_levels(rng, dims, cuts, low, largest):
    loudness, own = 1.0, jax.random.fold_in(rng, 6)
    for position, blocks in cuts:
        draws = jnp.exp(jax.random.uniform(jax.random.fold_in(own, position), (blocks,), jnp.float32, low / len(cuts), largest / len(cuts)))
        loudness = loudness * jnp.repeat(draws, dims[position] // blocks).reshape([-1 if axis == position else 1 for axis in range(len(dims))])
    return loudness


def scatter_about(stream_key, dims, deviation, most, shards=(), held_as=jnp.bfloat16):
    drawn = deviation * jax.random.normal(stream_key, dims, jnp.float32)
    if shards:
        drawn = drawn * shard_levels(stream_key, dims, shards, -0.22, 0.18)
    return jnp.clip(drawn, -most, most).astype(held_as)


def setup_inputs(seed: int = 0) -> dict:
    splits = jax.random.split(jax.random.key(seed), 6)
    return {
        "cotangent": draw_cotangent(jax.random.fold_in(splits[5], 71), 0),
        "activations": draw_activations(jax.random.fold_in(splits[5], 71), 0),
        "weight": scatter_about(splits[2], (FF, D), FF ** -0.5, 0.0390625, ((0, 32), (1, 8))),
        "row_prev": draw_row_prev(jax.random.fold_in(splits[5], 71), 0),
        "col_prev": draw_col_prev(jax.random.fold_in(splits[5], 71), 0),
    }


epsilon = 1e-30
decay_rate = 0.9

def reference(cotangent, activations, weight, row_prev, col_prev):

    def add_block(running, block_index):
        offset = block_index * BLOCK
        cot_block = lax.dynamic_slice_in_dim(cotangent, offset, BLOCK, 0)
        act_block = lax.dynamic_slice_in_dim(activations, offset, BLOCK, 0)
        return (running + jnp.dot(cot_block.T, act_block, preferred_element_type=jnp.float32), None)
    gradient, unused = lax.scan(add_block, jnp.zeros((FF, D), jnp.float32), jnp.arange(TOKENS // BLOCK, dtype=jnp.int32))
    input_grad = jnp.dot(cotangent, weight, preferred_element_type=jnp.float32).astype(jnp.bfloat16)
    square = gradient * gradient + epsilon
    row_stats = decay_rate * row_prev + (1.0 - decay_rate) * (lax.optimization_barrier(jnp.sum(square, axis=1)) / D)
    col_stats = decay_rate * col_prev + (1.0 - decay_rate) * (lax.optimization_barrier(jnp.sum(square, axis=0)) / FF)
    row_mean = jnp.sum(row_stats) / FF
    unclipped = gradient * lax.rsqrt(row_stats[:, None] * col_stats[None, :] / row_mean)
    root_mean = jnp.sqrt(jnp.sum(unclipped * unclipped) / (FF * D))
    update = unclipped / jnp.maximum(1.0, root_mean)
    return (input_grad, update)
```

```python
import jax
import jax.numpy as jnp
from jax import lax
from jax.experimental import pallas as pl
from jax.experimental.pallas import tpu as pltpu
from jax.sharding import Mesh
from jax.sharding import PartitionSpec as P

D = 6144
FF = 24576
HALF = 384

epsilon = 1e-30
decay_rate = 0.9


def exchange(value, axis, size, bit):
    return lax.ppermute(value, axis, [(i, i ^ bit) for i in range(size)])


def shift(value, axis, size, step):
    return lax.ppermute(value, axis, [(i, (i + step) % size) for i in range(size)])


def total(value, axis, size):
    bit = 1
    while bit < size:
        value = value + exchange(value, axis, size, bit)
        bit *= 2
    return value


def group_kernel(first, rows_ref, cores_ref, *refs):
    cots, owns, recvs = refs[0:4], refs[4:8], refs[8:12]
    keep_ref, send_ref = refs[12:14]
    if first:
        before_refs, outs = None, refs[14:]
    else:
        before_refs, outs = refs[14:16], refs[16:]
    grad_own, grad_recv, part_keep, part_send = outs
    cot = jnp.concatenate([c[...].reshape(256, 768) for c in cots], axis=0)
    for position, (acts, out) in enumerate(((owns, grad_own), (recvs, grad_recv))):
        act = jnp.concatenate([a[...].reshape(256, HALF) for a in acts], axis=0)
        term = lax.dot_general(cot, act, (((0,), (0,)), ((), ())), preferred_element_type=jnp.float32)
        out[...] = term if first else before_refs[position][...] + term
    for weight_ref, out in ((keep_ref, part_keep), (send_ref, part_send)):
        for j in range(4):
            part = jnp.dot(
                cots[j][...].reshape(256, 768), weight_ref[...], preferred_element_type=jnp.float32
            )
            out[:, j] = part.reshape(8, 32, HALF)


def group_call(rows, cores, cots, own, recv, keep, send, before=None):
    first = before is None
    whole = lambda shape: pl.BlockSpec(shape, lambda i, rows, cores: (0,) * len(shape))
    act_spec = lambda j: pl.BlockSpec((8, None, 32, HALF), lambda i, rows, cores: (0, rows[j], 0, 0))
    in_specs = [whole((8, 32, 768))] * 4
    in_specs += [act_spec(j) for j in range(4)] * 2
    in_specs += [whole((768, HALF))] * 2
    operands = list(cots) + [own] * 4 + [recv] * 4 + [keep, send]
    if not first:
        in_specs += [whole((768, HALF))] * 2
        operands += list(before)
    f32 = jnp.float32
    return pl.pallas_call(
        lambda *refs: group_kernel(first, *refs),
        grid_spec=pltpu.PrefetchScalarGridSpec(
            num_scalar_prefetch=2,
            grid=(1,),
            in_specs=in_specs,
            out_specs=[whole((768, HALF))] * 2 + [whole((8, 4, 32, HALF))] * 2,
        ),
        out_shape=[jax.ShapeDtypeStruct((768, HALF), f32)] * 2
        + [jax.ShapeDtypeStruct((8, 4, 32, HALF), f32)] * 2,
        compiler_params=pltpu.CompilerParams(vmem_limit_bytes=48 * 1024 * 1024),
        cost_estimate=pl.CostEstimate(
            flops=4 * 1024 * 768 * 768, bytes_accessed=14 * 1024 * 1024, transcendentals=0
        ),
    )(rows, cores, *operands)


def body(cotangent, activations, weight, row_prev, col_prev):
    x, yh, core = lax.axis_index("x"), lax.axis_index("yh"), lax.axis_index("core")
    yl = lax.axis_index("yl")

    own_cot = lax.all_to_all(cotangent, "z", 1, 0, tiled=True).reshape(8, 32, 768)
    other_cot = exchange(own_cot, "yh", 2, 1)
    right_cot = shift(own_cot, "x", 4, 1)
    left_cot = shift(own_cot, "x", 4, -1)
    far_cot = shift(own_cot, "x", 4, 2)
    other_right = shift(other_cot, "x", 4, 1)
    other_left = shift(other_cot, "x", 4, -1)
    other_far = exchange(far_cot, "yh", 2, 1)
    right, left, far = (x + 3) % 4, (x + 1) % 4, (x + 2) % 4
    rows_first = jnp.stack([x * 2 + yh, right * 2 + yh, left * 2 + yh, x * 2 + 1 - yh]).astype(jnp.int32)
    rows_second = jnp.stack(
        [far * 2 + yh, right * 2 + 1 - yh, left * 2 + 1 - yh, far * 2 + 1 - yh]
    ).astype(jnp.int32)
    cores = jnp.stack([core, 1 - core]).astype(jnp.int32)

    act_cols = lax.all_gather(activations, ("yl", "core"), axis=1, tiled=True)
    act_half = lax.dynamic_slice_in_dim(act_cols, core * HALF, HALF, 1)
    act_own = lax.all_gather(act_half, "z", axis=0, tiled=True).reshape(8, 8, 32, HALF)
    act_recv = exchange(act_own, "core", 2, 1)

    by_core = weight.reshape(768, 2, 2, 192)
    even = by_core[:, :, 0].reshape(768, HALF)
    odd = by_core[:, :, 1].reshape(768, HALF)
    keep = jnp.where(core == 0, even, odd)
    send = jnp.where(core == 0, odd, even)

    g_own, g_recv, keep_1, send_1 = group_call(
        rows_first, cores, [own_cot, right_cot, left_cot, other_cot], act_own, act_recv, keep, send
    )
    g_own, g_recv, keep_2, send_2 = group_call(
        rows_second,
        cores,
        [far_cot, other_right, other_left, other_far],
        act_own,
        act_recv,
        keep,
        send,
        (g_own, g_recv),
    )
    gradient = jnp.where(
        core == 0,
        jnp.concatenate([g_own, g_recv], axis=1),
        jnp.concatenate([g_recv, g_own], axis=1),
    )

    pieces = []
    for kept, sent in ((keep_1, send_1), (keep_2, send_2)):
        summed = kept + exchange(sent, "core", 2, 1)
        pieces.append(lax.psum_scatter(summed, "z", scatter_dimension=0, tiled=True).reshape(4, 32, HALF))
    summed = jnp.concatenate(pieces, axis=0)
    low, high = summed[:, :, :192], summed[:, :, 192:]
    mine = jnp.where(yl == 0, low, high)
    theirs = jnp.where(yl == 0, high, low)
    mine = (mine + exchange(theirs, "yl", 2, 1)).astype(jnp.bfloat16)
    rows = jnp.concatenate([rows_first, rows_second])
    input_grad = jnp.zeros((8, 32, 192), jnp.bfloat16)
    for j in range(8):
        input_grad = lax.dynamic_update_slice(input_grad, mine[j : j + 1], (rows[j], 0, 0))
    input_grad = input_grad.reshape(256, 192)

    square = gradient * gradient + epsilon
    row_sums = total(total(jnp.sum(square, axis=1), "x", 4), "yh", 2)
    row_stats = decay_rate * row_prev + (1.0 - decay_rate) * (row_sums / D)
    scaled = gradient * lax.rsqrt(row_stats)[:, None]
    sums = jnp.concatenate(
        [
            jnp.sum(square, axis=0),
            jnp.sum(scaled * scaled, axis=0),
            jnp.broadcast_to(jnp.sum(row_stats), (128,)),
        ]
    )
    sums = total(total(total(sums, "core", 2), "yl", 2), "z", 8)
    col_sums, scaled_sums, row_total = sums[:768], sums[768:1536], sums[1536]
    col_stats = decay_rate * col_prev + (1.0 - decay_rate) * (col_sums / FF)
    row_mean = row_total / FF
    part = jnp.sum(scaled_sums * row_mean / col_stats)
    squares_total = total(total(jnp.broadcast_to(part, (128,)), "x", 4), "yh", 2)[0]
    root_mean = jnp.sqrt(squares_total / (FF * D))
    unclipped = gradient * lax.rsqrt(row_stats[:, None] * col_stats[None, :] / row_mean)
    update = unclipped / jnp.maximum(1.0, root_mean)
    return (input_grad, update)


def solution(mesh):
    fine = Mesh(mesh.devices.reshape(4, 2, 2, 2, 8), ("x", "yh", "yl", "core", "z"))
    row, col = ("x", "yh"), ("yl", "core")
    return jax.shard_map(
        body,
        mesh=fine,
        in_specs=(
            P(("z",) + row, col),
            P("z", row + col),
            P(col + ("z",), row),
            P(col + ("z",)),
            P(row),
        ),
        out_specs=(P("z", row + col), P(col + ("z",), row)),
        check_vma=False,
    )
```

```python
import jax
import jax.numpy as jnp
from jax import lax
from jax.experimental import pallas as pl
from jax.experimental.pallas import tpu as pltpu
from jax.sharding import Mesh
from jax.sharding import PartitionSpec as P

D = 6144
FF = 24576
HALF = 384
STEP = 2
VMEM = 56 * 1024 * 1024

epsilon = 1e-30
decay_rate = 0.9


def exchange(value, axis, size, bit):
    return lax.ppermute(value, axis, [(i, i ^ bit) for i in range(size)])


def shift(value, axis, size, step):
    return lax.ppermute(value, axis, [(i, (i + step) % size) for i in range(size)])


def total(value, axis, size):
    bit = 1
    while bit < size:
        value = value + exchange(value, axis, size, bit)
        bit *= 2
    return value


def partial_kernel(cot_0, cot_1, cot_2, cot_3, keep_ref, send_ref, part_keep, part_send):
    for weight_ref, out in ((keep_ref, part_keep), (send_ref, part_send)):
        for j, cot in enumerate((cot_0, cot_1, cot_2, cot_3)):
            part = jnp.dot(
                cot[...].reshape(256, 768), weight_ref[...], preferred_element_type=jnp.float32
            )
            out[:, j] = part.reshape(8, 32, HALF)


def partial_call(cots, keep, send):
    return pl.pallas_call(
        partial_kernel,
        out_shape=[jax.ShapeDtypeStruct((8, 4, 32, HALF), jnp.float32)] * 2,
        compiler_params=pltpu.CompilerParams(vmem_limit_bytes=VMEM),
        cost_estimate=pl.CostEstimate(
            flops=2 * 1024 * 768 * 768,
            bytes_accessed=6 * 1024 * 1024,
            transcendentals=0,
        ),
    )(*cots, keep, send)


def gradient_kernel(rows_ref, halves_ref, *refs):
    cots, acts, out_ref = refs[:8], refs[8:10], refs[10]
    step = pl.program_id(0)
    cot = jnp.concatenate([c[...].reshape(STEP * 32, 768) for c in cots], axis=0)
    for h in range(2):
        act = jnp.concatenate(
            [acts[h][:, rows_ref[j]].reshape(STEP * 32, HALF) for j in range(8)], axis=0
        )
        term = lax.dot_general(cot, act, (((0,), (0,)), ((), ())), preferred_element_type=jnp.float32)
        columns = pl.ds(pl.multiple_of(halves_ref[h] * HALF, HALF), HALF)

        @pl.when(step == 0)
        def _():
            out_ref[:, columns] = term

        @pl.when(step > 0)
        def _():
            out_ref[:, columns] += term


def gradient_call(rows, halves, cots, acts):
    return pl.pallas_call(
        gradient_kernel,
        grid_spec=pltpu.PrefetchScalarGridSpec(
            num_scalar_prefetch=2,
            grid=(8 // STEP,),
            in_specs=[pl.BlockSpec((STEP, 32, 768), lambda s, rows, halves: (s, 0, 0))] * 8
            + [pl.BlockSpec((STEP, 8, 32, HALF), lambda s, rows, halves: (s, 0, 0, 0))] * 2,
            out_specs=pl.BlockSpec((768, 768), lambda s, rows, halves: (0, 0)),
        ),
        out_shape=jax.ShapeDtypeStruct((768, 768), jnp.float32),
        compiler_params=pltpu.CompilerParams(vmem_limit_bytes=VMEM),
        cost_estimate=pl.CostEstimate(
            flops=2 * 2048 * 768 * 768, bytes_accessed=9 * 1024 * 1024, transcendentals=0
        ),
    )(rows, halves, *cots, *acts)


def body(cotangent, activations, weight, row_prev, col_prev):
    x, yh, core = lax.axis_index("x"), lax.axis_index("yh"), lax.axis_index("core")
    yl = lax.axis_index("yl")

    act_cols = lax.all_gather(activations, ("yl", "core"), axis=1, tiled=True)
    act_half = lax.dynamic_slice_in_dim(act_cols, core * HALF, HALF, 1)
    act_half, cotangent = lax.optimization_barrier((act_half, cotangent))
    act_own = lax.all_gather(act_half, "z", axis=0, tiled=True).reshape(8, 8, 32, HALF)

    own_cot = lax.all_to_all(cotangent, "z", 1, 0, tiled=True).reshape(8, 32, 768)
    own_cot, weight = lax.optimization_barrier((own_cot, weight))
    other_cot = exchange(own_cot, "yh", 2, 1)
    right_cot = shift(own_cot, "x", 4, 1)
    left_cot = shift(own_cot, "x", 4, -1)
    far_cot = shift(own_cot, "x", 4, 2)
    other_right = shift(other_cot, "x", 4, 1)
    other_left = shift(other_cot, "x", 4, -1)
    other_far = exchange(far_cot, "yh", 2, 1)
    right, left, far = (x + 3) % 4, (x + 1) % 4, (x + 2) % 4
    rows = jnp.stack([x * 2 + yh, right * 2 + yh, left * 2 + yh, far * 2 + yh])
    rows = jnp.concatenate([rows, rows + 1 - 2 * yh]).astype(jnp.int32)
    halves = jnp.stack([core, 1 - core]).astype(jnp.int32)
    first = list(lax.optimization_barrier((own_cot, right_cot, left_cot, far_cot, other_right, other_left)))[:4]
    second = [other_cot, other_right, other_left, other_far]

    by_core = weight.reshape(768, 2, 2, 192)
    even = by_core[:, :, 0].reshape(768, HALF)
    odd = by_core[:, :, 1].reshape(768, HALF)
    keep = jnp.where(core == 0, even, odd)
    send = jnp.where(core == 0, odd, even)

    keep_1, send_1 = partial_call(first, keep, send)
    other_far, act_own = lax.optimization_barrier((other_far, act_own))
    second = [other_cot, other_right, other_left, other_far]
    keep_2, send_2 = partial_call(second, keep, send)
    send_2, act_own = lax.optimization_barrier((send_2, act_own))
    sent_2, act_recv = lax.optimization_barrier(
        (exchange(send_2, "core", 2, 1), exchange(act_own, "core", 2, 1))
    )
    gradient = gradient_call(rows, halves, first + second, [act_own, act_recv])

    summed = jnp.concatenate(
        [keep_1 + exchange(send_1, "core", 2, 1), keep_2 + sent_2], axis=1
    )
    summed = lax.psum_scatter(summed, "z", scatter_dimension=0, tiled=True).reshape(8, 32, HALF)
    low, high = summed[:, :, :192], summed[:, :, 192:]
    mine = jnp.where(yl == 0, low, high)
    theirs = jnp.where(yl == 0, high, low)
    mine = (mine + exchange(theirs, "yl", 2, 1)).astype(jnp.bfloat16)
    input_grad = jnp.zeros((8, 32, 192), jnp.bfloat16)
    for j in range(8):
        input_grad = lax.dynamic_update_slice(input_grad, mine[j : j + 1], (rows[j], 0, 0))
    input_grad = input_grad.reshape(256, 192)

    square = gradient * gradient + epsilon
    row_sums = total(total(jnp.sum(square, axis=1), "x", 4), "yh", 2)
    row_stats = decay_rate * row_prev + (1.0 - decay_rate) * (row_sums / D)
    scaled = gradient * lax.rsqrt(row_stats)[:, None]
    sums = jnp.concatenate(
        [
            jnp.sum(square, axis=0),
            jnp.sum(scaled * scaled, axis=0),
            jnp.broadcast_to(jnp.sum(row_stats), (128,)),
        ]
    )
    sums = total(total(total(sums, "core", 2), "yl", 2), "z", 8)
    col_sums, scaled_sums, row_total = sums[:768], sums[768:1536], sums[1536]
    col_stats = decay_rate * col_prev + (1.0 - decay_rate) * (col_sums / FF)
    row_mean = row_total / FF
    part = jnp.sum(scaled_sums * row_mean / col_stats)
    squares_total = total(total(jnp.broadcast_to(part, (128,)), "x", 4), "yh", 2)[0]
    root_mean = jnp.sqrt(squares_total / (FF * D))
    unclipped = gradient * lax.rsqrt(row_stats[:, None] * col_stats[None, :] / row_mean)
    update = unclipped / jnp.maximum(1.0, root_mean)
    return (input_grad, update)


def solution(mesh):
    fine = Mesh(mesh.devices.reshape(4, 2, 2, 2, 8), ("x", "yh", "yl", "core", "z"))
    row, col = ("x", "yh"), ("yl", "core")
    return jax.shard_map(
        body,
        mesh=fine,
        in_specs=(
            P(("z",) + row, col),
            P("z", row + col),
            P(col + ("z",), row),
            P(col + ("z",)),
            P(row),
        ),
        out_specs=(P("z", row + col), P(col + ("z",), row)),
        check_vma=False,
    )
```

```python
import jax
import jax.numpy as jnp
from jax import lax
from jax.experimental import pallas as pl
from jax.experimental.pallas import tpu as pltpu
from jax.sharding import Mesh
from jax.sharding import PartitionSpec as P

D = 6144
FF = 24576
HALF = 384
VMEM = 56 * 1024 * 1024

epsilon = 1e-30
decay_rate = 0.9


def exchange(value, axis, size, bit):
    return lax.ppermute(value, axis, [(i, i ^ bit) for i in range(size)])


def shift(value, axis, size, step):
    return lax.ppermute(value, axis, [(i, (i + step) % size) for i in range(size)])


def total(value, axis, size):
    bit = 1
    while bit < size:
        value = value + exchange(value, axis, size, bit)
        bit *= 2
    return value


def tokens(refs, count):
    return jnp.concatenate([ref[...].reshape(count * 32, 768) for ref in refs], axis=0)


def product(cot, weight_ref):
    return jnp.dot(cot, weight_ref[...], preferred_element_type=jnp.float32)


def split(part, count):
    return [part[j * count * 32 : (j + 1) * count * 32].reshape(count, 32, HALF) for j in range(4)]


def first_kernel(*refs):
    cots, (keep_ref, send_ref, part_keep, part_send) = refs[:4], refs[4:]
    cot = tokens(cots, 2)
    for weight_ref, out in ((keep_ref, part_keep), (send_ref, part_send)):
        for j, part in enumerate(split(product(cot, weight_ref), 2)):
            out[:, j] = part


def second_kernel(rows_ref, *refs):
    cots, others = refs[:4], refs[4:8]
    keep_ref, other_ref, before_ref, recv_ref, out = refs[8:]
    whole = product(tokens(cots, 2), keep_ref) + product(tokens(others, 2), other_ref)
    for j, part in enumerate(split(whole, 2)):
        out[:, rows_ref[j]] = before_ref[:, j] + recv_ref[:, j]
        out[:, rows_ref[4 + j]] = part


COT = pl.BlockSpec((2, 32, 768), lambda s, *_: (s, 0, 0))
WEIGHT = pl.BlockSpec((768, HALF), lambda s, *_: (0, 0))
PART = pl.BlockSpec((2, 4, 32, HALF), lambda s, *_: (s, 0, 0, 0))


def first_call(cots, keep, send):
    return pl.pallas_call(
        first_kernel,
        grid=(4,),
        in_specs=[COT] * 4 + [WEIGHT] * 2,
        out_specs=[PART] * 2,
        out_shape=[jax.ShapeDtypeStruct((8, 4, 32, HALF), jnp.float32)] * 2,
        compiler_params=pltpu.CompilerParams(vmem_limit_bytes=VMEM),
        cost_estimate=pl.CostEstimate(
            flops=2 * 1024 * 768 * 768, bytes_accessed=6 * 1024 * 1024, transcendentals=0
        ),
    )(*cots, keep, send)


def second_call(rows, cots, others, keep, other, before, received):
    return pl.pallas_call(
        second_kernel,
        grid_spec=pltpu.PrefetchScalarGridSpec(
            num_scalar_prefetch=1,
            grid=(4,),
            in_specs=[COT] * 8 + [WEIGHT] * 2 + [PART] * 2,
            out_specs=pl.BlockSpec((2, 8, 32, HALF), lambda s, rows: (s, 0, 0, 0)),
        ),
        out_shape=jax.ShapeDtypeStruct((8, 8, 32, HALF), jnp.float32),
        compiler_params=pltpu.CompilerParams(vmem_limit_bytes=VMEM),
        cost_estimate=pl.CostEstimate(
            flops=2 * 1024 * 768 * 768, bytes_accessed=10 * 1024 * 1024, transcendentals=0
        ),
    )(rows, *cots, *others, keep, other, before, received)


STEP = 4


def gradient_kernel(rows_ref, halves_ref, *refs):
    cots, acts, (out_ref, row_ref, col_ref) = refs[:8], refs[8:10], refs[10:]
    step = pl.program_id(0)
    act = jnp.concatenate(
        [
            jnp.concatenate([a[:, rows_ref[j]].reshape(STEP * 32, HALF) for j in range(8)], axis=0)
            for a in acts
        ],
        axis=1,
    )
    term = lax.dot_general(
        tokens(cots, STEP), act, (((0,), (0,)), ((), ())), preferred_element_type=jnp.float32
    )
    for h in range(2):
        columns = pl.ds(pl.multiple_of(halves_ref[h] * HALF, HALF), HALF)
        part = term[:, h * HALF : (h + 1) * HALF]

        @pl.when(step == 0)
        def _():
            out_ref[:, columns] = part

        @pl.when(step > 0)
        def _():
            out_ref[:, columns] += part

    @pl.when(step == 8 // STEP - 1)
    def _():
        gradient = out_ref[...]
        square = gradient * gradient + epsilon
        col_ref[...] = jnp.sum(square, axis=0)
        lanes = sum(square[:, k * 128 : (k + 1) * 128] for k in range(6))
        row_ref[...] = jnp.sum(lanes.T, axis=0)


def gradient_call(rows, halves, cots, acts):
    vector = pl.BlockSpec((768,), lambda s, rows, halves: (0,))
    return pl.pallas_call(
        gradient_kernel,
        grid_spec=pltpu.PrefetchScalarGridSpec(
            num_scalar_prefetch=2,
            grid=(8 // STEP,),
            in_specs=[pl.BlockSpec((STEP, 32, 768), lambda s, rows, halves: (s, 0, 0))] * 8
            + [pl.BlockSpec((STEP, 8, 32, HALF), lambda s, rows, halves: (s, 0, 0, 0))] * 2,
            out_specs=[pl.BlockSpec((768, 768), lambda s, rows, halves: (0, 0)), vector, vector],
        ),
        out_shape=[
            jax.ShapeDtypeStruct((768, 768), jnp.float32),
            jax.ShapeDtypeStruct((768,), jnp.float32),
            jax.ShapeDtypeStruct((768,), jnp.float32),
        ],
        compiler_params=pltpu.CompilerParams(vmem_limit_bytes=VMEM),
        cost_estimate=pl.CostEstimate(
            flops=2 * 2048 * 768 * 768, bytes_accessed=9 * 1024 * 1024, transcendentals=0
        ),
    )(rows, halves, *cots, *acts)


def body(cotangent, activations, weight, row_prev, col_prev):
    x, yh, core = lax.axis_index("x"), lax.axis_index("yh"), lax.axis_index("core")
    yl = lax.axis_index("yl")

    act_cols = lax.all_gather(activations, ("yl", "core"), axis=1, tiled=True)
    act_half = lax.dynamic_slice_in_dim(act_cols, core * HALF, HALF, 1)
    act_half, cotangent = lax.optimization_barrier((act_half, cotangent))
    act_own = lax.all_gather(act_half, "z", axis=0, tiled=True).reshape(8, 8, 32, HALF)

    own_cot = lax.all_to_all(cotangent, "z", 1, 0, tiled=True).reshape(8, 32, 768)
    own_cot, weight = lax.optimization_barrier((own_cot, weight))
    other_cot = exchange(own_cot, "yh", 2, 1)
    right_cot = shift(own_cot, "x", 4, 1)
    left_cot = shift(own_cot, "x", 4, -1)
    far_cot = shift(own_cot, "x", 4, 2)
    other_right = shift(other_cot, "x", 4, 1)
    other_left = shift(other_cot, "x", 4, -1)
    other_far = exchange(far_cot, "yh", 2, 1)
    right, left, far = (x + 3) % 4, (x + 1) % 4, (x + 2) % 4
    rows = jnp.stack([x * 2 + yh, right * 2 + yh, left * 2 + yh, far * 2 + yh])
    rows = jnp.concatenate([rows, rows + 1 - 2 * yh]).astype(jnp.int32)
    halves = jnp.stack([core, 1 - core]).astype(jnp.int32)
    first = [own_cot, right_cot, left_cot, far_cot]
    second = [other_cot, other_right, other_left, other_far]

    by_core = weight.reshape(768, 2, 2, 192)
    even = by_core[:, :, 0].reshape(768, HALF)
    odd = by_core[:, :, 1].reshape(768, HALF)
    keep = jnp.where(core == 0, even, odd)
    send = jnp.where(core == 0, odd, even)

    other_keep = exchange(send, "core", 2, 1)

    others = [exchange(cot, "core", 2, 1) for cot in second[:3]]
    *arrived, keep, send, other_keep, act_own = lax.optimization_barrier(
        (*first, *second, *others, keep, send, other_keep, act_own)
    )
    first, second, others = arrived[:4], arrived[4:8], arrived[8:]
    act_recv = exchange(act_own, "core", 2, 1)
    keep_1, send_1 = first_call(first, keep, send)
    recv_1 = exchange(send_1, "core", 2, 1)
    gradient, row_sums, col_sums = gradient_call(rows, halves, first + second, [act_own, act_recv])

    others.append(exchange(second[3], "core", 2, 1))
    row_sums = row_sums + exchange(row_sums, "x", 4, 1)
    others[0], row_sums = lax.optimization_barrier((others[0], row_sums))
    summed = second_call(rows, second, others, keep, other_keep, keep_1, recv_1)
    summed = lax.psum_scatter(summed, "z", scatter_dimension=0, tiled=True).reshape(8, 32, HALF)
    low, high = summed[:, :, :192], summed[:, :, 192:]
    mine = jnp.where(yl == 0, low, high)
    theirs = jnp.where(yl == 0, high, low)
    mine = (mine + exchange(theirs, "yl", 2, 1)).astype(jnp.bfloat16)
    input_grad = mine.reshape(256, 192)

    row_sums = total(row_sums + exchange(row_sums, "x", 4, 2), "yh", 2)
    row_stats = decay_rate * row_prev + (1.0 - decay_rate) * (row_sums / D)
    scaled = gradient * lax.rsqrt(row_stats)[:, None]
    sums = jnp.concatenate(
        [
            col_sums,
            jnp.sum(scaled * scaled, axis=0),
            jnp.broadcast_to(jnp.sum(row_stats), (768,)),
        ]
    )
    sums = total(total(total(sums, "core", 2), "yl", 2), "z", 8)
    col_sums, scaled_sums, row_mean = sums[:768], sums[768:1536], sums[1536:] / FF
    col_stats = decay_rate * col_prev + (1.0 - decay_rate) * (col_sums / FF)
    part = jnp.sum((scaled_sums * row_mean / col_stats).reshape(6, 128), axis=0)
    part = total(total(part, "x", 4), "yh", 2)
    part, input_grad = lax.optimization_barrier((part, input_grad))
    squares_total = jnp.sum(part)
    root_mean = jnp.sqrt(squares_total / (FF * D))
    unclipped = gradient * lax.rsqrt(row_stats[:, None] * col_stats[None, :] / row_mean[None, :])
    update = unclipped / jnp.maximum(1.0, root_mean)
    return (input_grad, update)


def solution(mesh):
    fine = Mesh(mesh.devices.reshape(4, 2, 2, 2, 8), ("x", "yh", "yl", "core", "z"))
    row, col = ("x", "yh"), ("yl", "core")
    return jax.shard_map(
        body,
        mesh=fine,
        in_specs=(
            P(("z",) + row, col),
            P("z", row + col),
            P(col + ("z",), row),
            P(col + ("z",)),
            P(row),
        ),
        out_specs=(P("z", row + col), P(col + ("z",), row)),
        check_vma=False,
    )
```

```python
import jax
import jax.numpy as jnp
from jax import lax
from jax.experimental import pallas as pl
from jax.experimental.pallas import tpu as pltpu
from jax.sharding import Mesh
from jax.sharding import PartitionSpec as P

D = 6144
FF = 24576
HALF = 384
FIRST, SECOND = 3, 5
VMEM = 56 * 1024 * 1024

epsilon = 1e-30
decay_rate = 0.9


def exchange(value, axis, size, bit):
    return lax.ppermute(value, axis, [(i, i ^ bit) for i in range(size)])


def shift(value, axis, size, step):
    return lax.ppermute(value, axis, [(i, (i + step) % size) for i in range(size)])


def total(value, axis, size):
    bit = 1
    while bit < size:
        value = value + exchange(value, axis, size, bit)
        bit *= 2
    return value


def tokens(refs, count):
    return jnp.concatenate([ref[...].reshape(count * 32, 768) for ref in refs], axis=0)


def product(cot, weight_ref):
    return jnp.dot(cot, weight_ref[...], preferred_element_type=jnp.float32)


def split(part, count):
    rows = count * 32
    return [part[k : k + rows].reshape(count, 32, HALF) for k in range(0, part.shape[0], rows)]


def first_kernel(*refs):
    cots, (keep_ref, send_ref, part_keep, part_send) = refs[:FIRST], refs[FIRST:]
    cot = tokens(cots, 2)
    for weight_ref, out in ((keep_ref, part_keep), (send_ref, part_send)):
        for j, part in enumerate(split(product(cot, weight_ref), 2)):
            out[:, j] = part


def second_kernel(rows_ref, *refs):
    cots, others = refs[:SECOND], refs[SECOND : 2 * SECOND]
    keep_ref, other_ref, before_ref, recv_ref, out = refs[2 * SECOND :]
    whole = product(tokens(cots, 2), keep_ref) + product(tokens(others, 2), other_ref)
    for j in range(FIRST):
        out[:, rows_ref[j]] = before_ref[:, j] + recv_ref[:, j]
    for j, part in enumerate(split(whole, 2)):
        out[:, rows_ref[FIRST + j]] = part


COT = pl.BlockSpec((2, 32, 768), lambda s, *_: (s, 0, 0))
WEIGHT = pl.BlockSpec((768, HALF), lambda s, *_: (0, 0))
PART = pl.BlockSpec((2, FIRST, 32, HALF), lambda s, *_: (s, 0, 0, 0))


def first_call(cots, keep, send):
    return pl.pallas_call(
        first_kernel,
        grid=(4,),
        in_specs=[COT] * FIRST + [WEIGHT] * 2,
        out_specs=[PART] * 2,
        out_shape=[jax.ShapeDtypeStruct((8, FIRST, 32, HALF), jnp.float32)] * 2,
        compiler_params=pltpu.CompilerParams(vmem_limit_bytes=VMEM),
        cost_estimate=pl.CostEstimate(
            flops=2 * 1024 * 768 * 768, bytes_accessed=6 * 1024 * 1024, transcendentals=0
        ),
    )(*cots, keep, send)


def second_call(rows, cots, others, keep, other, before, received):
    return pl.pallas_call(
        second_kernel,
        grid_spec=pltpu.PrefetchScalarGridSpec(
            num_scalar_prefetch=1,
            grid=(4,),
            in_specs=[COT] * 2 * SECOND + [WEIGHT] * 2 + [PART] * 2,
            out_specs=pl.BlockSpec((2, 8, 32, HALF), lambda s, rows: (s, 0, 0, 0)),
        ),
        out_shape=jax.ShapeDtypeStruct((8, 8, 32, HALF), jnp.float32),
        compiler_params=pltpu.CompilerParams(vmem_limit_bytes=VMEM),
        cost_estimate=pl.CostEstimate(
            flops=2 * 1024 * 768 * 768, bytes_accessed=10 * 1024 * 1024, transcendentals=0
        ),
    )(rows, *cots, *others, keep, other, before, received)


STEP = 4


def gradient_kernel(rows_ref, halves_ref, *refs):
    cots, acts, (out_ref, row_ref, col_ref) = refs[:8], refs[8:10], refs[10:]
    step = pl.program_id(0)
    act = jnp.concatenate(
        [
            jnp.concatenate([a[:, rows_ref[j]].reshape(STEP * 32, HALF) for j in range(8)], axis=0)
            for a in acts
        ],
        axis=1,
    )
    term = lax.dot_general(
        tokens(cots, STEP), act, (((0,), (0,)), ((), ())), preferred_element_type=jnp.float32
    )
    for h in range(2):
        columns = pl.ds(pl.multiple_of(halves_ref[h] * HALF, HALF), HALF)
        part = term[:, h * HALF : (h + 1) * HALF]

        @pl.when(step == 0)
        def _():
            out_ref[:, columns] = part

        @pl.when(step > 0)
        def _():
            out_ref[:, columns] += part

    @pl.when(step == 8 // STEP - 1)
    def _():
        gradient = out_ref[...]
        square = gradient * gradient + epsilon
        col_ref[...] = jnp.sum(square, axis=0)
        lanes = sum(square[:, k * 128 : (k + 1) * 128] for k in range(6))
        row_ref[...] = jnp.sum(lanes.T, axis=0)


def gradient_call(rows, halves, cots, acts):
    vector = pl.BlockSpec((768,), lambda s, rows, halves: (0,))
    return pl.pallas_call(
        gradient_kernel,
        grid_spec=pltpu.PrefetchScalarGridSpec(
            num_scalar_prefetch=2,
            grid=(8 // STEP,),
            in_specs=[pl.BlockSpec((STEP, 32, 768), lambda s, rows, halves: (s, 0, 0))] * 8
            + [pl.BlockSpec((STEP, 8, 32, HALF), lambda s, rows, halves: (s, 0, 0, 0))] * 2,
            out_specs=[pl.BlockSpec((768, 768), lambda s, rows, halves: (0, 0)), vector, vector],
        ),
        out_shape=[
            jax.ShapeDtypeStruct((768, 768), jnp.float32),
            jax.ShapeDtypeStruct((768,), jnp.float32),
            jax.ShapeDtypeStruct((768,), jnp.float32),
        ],
        compiler_params=pltpu.CompilerParams(vmem_limit_bytes=VMEM),
        cost_estimate=pl.CostEstimate(
            flops=2 * 2048 * 768 * 768, bytes_accessed=9 * 1024 * 1024, transcendentals=0
        ),
    )(rows, halves, *cots, *acts)


def body(cotangent, activations, weight, row_prev, col_prev):
    x, yh, core = lax.axis_index("x"), lax.axis_index("yh"), lax.axis_index("core")
    yl = lax.axis_index("yl")

    act_cols = lax.all_gather(activations, ("yl", "core"), axis=1, tiled=True)
    act_half = lax.dynamic_slice_in_dim(act_cols, core * HALF, HALF, 1)
    act_half, cotangent = lax.optimization_barrier((act_half, cotangent))
    act_own = lax.all_gather(act_half, "z", axis=0, tiled=True).reshape(8, 8, 32, HALF)

    own_cot = lax.all_to_all(cotangent, "z", 1, 0, tiled=True).reshape(8, 32, 768)
    own_cot, weight = lax.optimization_barrier((own_cot, weight))
    other_cot = exchange(own_cot, "yh", 2, 1)
    right_cot = shift(own_cot, "x", 4, 1)
    left_cot = shift(own_cot, "x", 4, -1)
    far_cot = shift(own_cot, "x", 4, 2)
    other_right = shift(other_cot, "x", 4, 1)
    other_left = shift(other_cot, "x", 4, -1)
    other_far = exchange(far_cot, "yh", 2, 1)
    right, left, far = (x + 3) % 4, (x + 1) % 4, (x + 2) % 4
    columns = [x, x, far, right, left, right, left, far]
    sides = [yh, 1 - yh, yh, yh, yh, 1 - yh, 1 - yh, 1 - yh]
    rows = jnp.stack([c * 2 + side for c, side in zip(columns, sides)]).astype(jnp.int32)
    halves = jnp.stack([core, 1 - core]).astype(jnp.int32)
    first = [own_cot, other_cot, far_cot]
    second = [right_cot, left_cot, other_right, other_left, other_far]

    by_core = weight.reshape(768, 2, 2, 192)
    even = by_core[:, :, 0].reshape(768, HALF)
    odd = by_core[:, :, 1].reshape(768, HALF)
    keep = jnp.where(core == 0, even, odd)
    send = jnp.where(core == 0, odd, even)

    keep_1, send_1 = first_call(first, keep, send)
    others = [exchange(cot, "core", 2, 1) for cot in second[:2]]
    *arrived, keep, send, keep_1, send_1, rows, halves, act_own = lax.optimization_barrier(
        (*first, *second, *others, keep, send, keep_1, send_1, rows, halves, act_own)
    )
    first, second, others = arrived[:FIRST], arrived[FIRST:8], arrived[8:]
    act_recv = exchange(act_own, "core", 2, 1)
    recv_1 = exchange(send_1, "core", 2, 1)
    other_keep = exchange(send, "core", 2, 1)
    gradient, row_sums, col_sums = gradient_call(rows, halves, first + second, [act_own, act_recv])

    others += [exchange(cot, "core", 2, 1) for cot in second[2:]]
    row_sums = row_sums + exchange(row_sums, "x", 4, 1)
    others[0], row_sums = lax.optimization_barrier((others[0], row_sums))
    summed = second_call(rows, second, others, keep, other_keep, keep_1, recv_1)
    summed = lax.psum_scatter(summed, "z", scatter_dimension=0, tiled=True)

    row_sums = total(row_sums + exchange(row_sums, "x", 4, 2), "yh", 2)
    row_stats = decay_rate * row_prev + (1.0 - decay_rate) * (row_sums / D)
    scaled = gradient * lax.rsqrt(row_stats)[:, None]
    sums = jnp.concatenate(
        [
            col_sums,
            jnp.sum(scaled * scaled, axis=0),
            jnp.broadcast_to(jnp.sum(row_stats), (768,)),
        ]
    )
    sums = total(total(total(sums, "core", 2), "yl", 2), "z", 8)
    col_sums, scaled_sums, row_mean = sums[:768], sums[768:1536], sums[1536:] / FF
    col_stats = decay_rate * col_prev + (1.0 - decay_rate) * (col_sums / FF)
    part = jnp.sum((scaled_sums * row_mean / col_stats).reshape(6, 128), axis=0)
    part = part + exchange(part, "x", 4, 1)
    part, summed = lax.optimization_barrier((part, summed))
    part = total(part + exchange(part, "x", 4, 2), "yh", 2)

    summed = summed.reshape(8, 32, HALF)
    low, high = summed[:, :, :192], summed[:, :, 192:]
    mine = jnp.where(yl == 0, low, high)
    theirs = jnp.where(yl == 0, high, low)
    mine = (mine + exchange(theirs, "yl", 2, 1)).astype(jnp.bfloat16)
    input_grad = mine.reshape(256, 192)
    part, input_grad = lax.optimization_barrier((part, input_grad))

    squares_total = jnp.sum(part)
    root_mean = jnp.sqrt(squares_total / (FF * D))
    unclipped = gradient * lax.rsqrt(row_stats[:, None] * col_stats[None, :] / row_mean[None, :])
    update = unclipped / jnp.maximum(1.0, root_mean)
    return (input_grad, update)


def solution(mesh):
    fine = Mesh(mesh.devices.reshape(4, 2, 2, 2, 8), ("x", "yh", "yl", "core", "z"))
    row, col = ("x", "yh"), ("yl", "core")
    return jax.shard_map(
        body,
        mesh=fine,
        in_specs=(
            P(("z",) + row, col),
            P("z", row + col),
            P(col + ("z",), row),
            P(col + ("z",)),
            P(row),
        ),
        out_specs=(P("z", row + col), P(col + ("z",), row)),
        check_vma=False,
    )
```

```python
import jax
import jax.numpy as jnp
from jax import lax
from jax.experimental import pallas as pl
from jax.experimental.pallas import tpu as pltpu
from jax.sharding import Mesh
from jax.sharding import PartitionSpec as P

D = 6144
FF = 24576
HALF = 384
FIRST, SECOND = 3, 5
VMEM = 56 * 1024 * 1024

epsilon = 1e-30
decay_rate = 0.9


def exchange(value, axis, size, bit):
    return lax.ppermute(value, axis, [(i, i ^ bit) for i in range(size)])


def shift(value, axis, size, step):
    return lax.ppermute(value, axis, [(i, (i + step) % size) for i in range(size)])


def total(value, axis, size):
    bit = 1
    while bit < size:
        value = value + exchange(value, axis, size, bit)
        bit *= 2
    return value


def reduce_four(value, axis, size, bits):
    others = [exchange(value, axis, size, bit) for bit in bits]
    for other in others:
        value = value + other
    return value


def weight_kernel(core_ref, weight_ref, keep_ref, send_ref):
    weight = weight_ref[...]
    even = jnp.concatenate([weight[:, :192], weight[:, HALF : HALF + 192]], axis=1)
    odd = jnp.concatenate([weight[:, 192:HALF], weight[:, HALF + 192 :]], axis=1)
    first = core_ref[0] == 0
    keep_ref[...] = jnp.where(first, even, odd)
    send_ref[...] = jnp.where(first, odd, even)


def weight_call(halves, weight):
    spec = pl.BlockSpec((256, HALF), lambda s, halves: (s, 0))
    return pl.pallas_call(
        weight_kernel,
        grid_spec=pltpu.PrefetchScalarGridSpec(
            num_scalar_prefetch=1,
            grid=(3,),
            in_specs=[pl.BlockSpec((256, 768), lambda s, halves: (s, 0))],
            out_specs=[spec, spec],
        ),
        out_shape=[jax.ShapeDtypeStruct((768, HALF), jnp.bfloat16)] * 2,
        compiler_params=pltpu.CompilerParams(vmem_limit_bytes=VMEM),
    )(halves, weight)


def tokens(refs, count):
    return jnp.concatenate([ref[...].reshape(count * 32, 768) for ref in refs], axis=0)


def product(cot, weight_ref):
    return jnp.dot(cot, weight_ref[...], preferred_element_type=jnp.float32)


def split(part, count):
    rows = count * 32
    return [part[k : k + rows].reshape(count, 32, HALF) for k in range(0, part.shape[0], rows)]


def first_kernel(*refs):
    cots, (keep_ref, send_ref, part_keep, part_send) = refs[:FIRST], refs[FIRST:]
    cot = tokens(cots, 2)
    for weight_ref, out in ((keep_ref, part_keep), (send_ref, part_send)):
        for j, part in enumerate(split(product(cot, weight_ref), 2)):
            out[:, j] = part


def second_kernel(rows_ref, *refs):
    cots, others = refs[:SECOND], refs[SECOND : 2 * SECOND]
    keep_ref, other_ref, before_ref, recv_ref, out = refs[2 * SECOND :]
    whole = product(tokens(cots, 2), keep_ref) + product(tokens(others, 2), other_ref)
    for j in range(FIRST):
        out[:, rows_ref[j]] = before_ref[:, j] + recv_ref[:, j]
    for j, part in enumerate(split(whole, 2)):
        out[:, rows_ref[FIRST + j]] = part


COT = pl.BlockSpec((2, 32, 768), lambda s, *_: (s, 0, 0))
WEIGHT = pl.BlockSpec((768, HALF), lambda s, *_: (0, 0))
PART = pl.BlockSpec((2, FIRST, 32, HALF), lambda s, *_: (s, 0, 0, 0))


def first_call(cots, keep, send):
    return pl.pallas_call(
        first_kernel,
        grid=(4,),
        in_specs=[COT] * FIRST + [WEIGHT] * 2,
        out_specs=[PART] * 2,
        out_shape=[jax.ShapeDtypeStruct((8, FIRST, 32, HALF), jnp.float32)] * 2,
        compiler_params=pltpu.CompilerParams(vmem_limit_bytes=VMEM),
        cost_estimate=pl.CostEstimate(
            flops=2 * 1024 * 768 * 768, bytes_accessed=6 * 1024 * 1024, transcendentals=0
        ),
    )(*cots, keep, send)


def second_call(rows, cots, others, keep, other, before, received):
    return pl.pallas_call(
        second_kernel,
        grid_spec=pltpu.PrefetchScalarGridSpec(
            num_scalar_prefetch=1,
            grid=(4,),
            in_specs=[COT] * 2 * SECOND + [WEIGHT] * 2 + [PART] * 2,
            out_specs=pl.BlockSpec((2, 8, 32, HALF), lambda s, rows: (s, 0, 0, 0)),
        ),
        out_shape=jax.ShapeDtypeStruct((8, 8, 32, HALF), jnp.float32),
        compiler_params=pltpu.CompilerParams(vmem_limit_bytes=VMEM),
        cost_estimate=pl.CostEstimate(
            flops=2 * 1024 * 768 * 768, bytes_accessed=10 * 1024 * 1024, transcendentals=0
        ),
    )(rows, *cots, *others, keep, other, before, received)


STEP = 4


def gradient_kernel(rows_ref, halves_ref, *refs):
    cots, acts, (out_ref, row_ref, col_ref) = refs[:8], refs[8:10], refs[10:]
    step = pl.program_id(0)
    act = jnp.concatenate(
        [
            jnp.concatenate([a[:, rows_ref[j]].reshape(STEP * 32, HALF) for j in range(8)], axis=0)
            for a in acts
        ],
        axis=1,
    )
    term = lax.dot_general(
        tokens(cots, STEP), act, (((0,), (0,)), ((), ())), preferred_element_type=jnp.float32
    )
    for h in range(2):
        columns = pl.ds(pl.multiple_of(halves_ref[h] * HALF, HALF), HALF)
        part = term[:, h * HALF : (h + 1) * HALF]

        @pl.when(step == 0)
        def _():
            out_ref[:, columns] = part

        @pl.when(step > 0)
        def _():
            out_ref[:, columns] += part

    @pl.when(step == 8 // STEP - 1)
    def _():
        gradient = out_ref[...]
        square = gradient * gradient + epsilon
        col_ref[...] = jnp.sum(square, axis=0)
        lanes = sum(square[:, k * 128 : (k + 1) * 128] for k in range(6))
        row_ref[...] = jnp.sum(lanes.T, axis=0)


def gradient_call(rows, halves, cots, acts):
    vector = pl.BlockSpec((768,), lambda s, rows, halves: (0,))
    return pl.pallas_call(
        gradient_kernel,
        grid_spec=pltpu.PrefetchScalarGridSpec(
            num_scalar_prefetch=2,
            grid=(8 // STEP,),
            in_specs=[pl.BlockSpec((STEP, 32, 768), lambda s, rows, halves: (s, 0, 0))] * 8
            + [pl.BlockSpec((STEP, 8, 32, HALF), lambda s, rows, halves: (s, 0, 0, 0))] * 2,
            out_specs=[pl.BlockSpec((768, 768), lambda s, rows, halves: (0, 0)), vector, vector],
        ),
        out_shape=[
            jax.ShapeDtypeStruct((768, 768), jnp.float32),
            jax.ShapeDtypeStruct((768,), jnp.float32),
            jax.ShapeDtypeStruct((768,), jnp.float32),
        ],
        compiler_params=pltpu.CompilerParams(vmem_limit_bytes=VMEM),
        cost_estimate=pl.CostEstimate(
            flops=2 * 2048 * 768 * 768, bytes_accessed=9 * 1024 * 1024, transcendentals=0
        ),
    )(rows, halves, *cots, *acts)


def body(cotangent, activations, weight, row_prev, col_prev):
    x, yh, core = lax.axis_index("x"), lax.axis_index("yh"), lax.axis_index("core")
    yl = lax.axis_index("yl")

    act_cols = lax.all_gather(activations, ("yl", "core"), axis=1, tiled=True)
    act_half = lax.dynamic_slice_in_dim(act_cols, core * HALF, HALF, 1)
    act_half, cotangent = lax.optimization_barrier((act_half, cotangent))
    act_own = lax.all_gather(act_half, "z", axis=0, tiled=True).reshape(8, 8, 32, HALF)

    own_cot = lax.all_to_all(cotangent, "z", 1, 0, tiled=True).reshape(8, 32, 768)
    own_cot, weight = lax.optimization_barrier((own_cot, weight))
    right, left, far = (x + 3) % 4, (x + 1) % 4, (x + 2) % 4
    columns = [x, x, far, right, left, far, right, left]
    sides = [yh, 1 - yh, yh, yh, yh, 1 - yh, 1 - yh, 1 - yh]
    rows = jnp.stack([c * 2 + side for c, side in zip(columns, sides)]).astype(jnp.int32)
    halves = jnp.stack([core, 1 - core]).astype(jnp.int32)
    keep, send = weight_call(halves, weight)

    other_cot = exchange(own_cot, "yh", 2, 1)
    other_cot, keep, send, rows, halves = lax.optimization_barrier((other_cot, keep, send, rows, halves))
    right_cot = shift(own_cot, "x", 4, 1)
    left_cot = shift(own_cot, "x", 4, -1)
    far_cot = shift(own_cot, "x", 4, 2)
    other_right = shift(other_cot, "x", 4, 1)
    other_left = shift(other_cot, "x", 4, -1)
    other_far = exchange(far_cot, "yh", 2, 1)
    first = [own_cot, other_cot, far_cot]
    second = [right_cot, left_cot, other_far, other_right, other_left]

    keep_1, send_1 = first_call(first, keep, send)
    keep_1, send_1, *second[:2] = lax.optimization_barrier((keep_1, send_1, *second[:2]))
    others = [exchange(cot, "core", 2, 1) for cot in second[:5]]
    other_keep = exchange(send, "core", 2, 1)
    *arrived, other_keep, keep_1, send_1, act_own = lax.optimization_barrier(
        (*first, *second, *others, other_keep, keep_1, send_1, act_own)
    )
    first, second, others = arrived[:FIRST], arrived[FIRST:8], arrived[8:]
    recv_1 = exchange(send_1, "core", 2, 1)
    others += [exchange(cot, "core", 2, 1) for cot in second[5:]]
    act_recv = exchange(act_own, "core", 2, 1)
    summed = second_call(rows, second, others, keep, other_keep, keep_1, recv_1)
    summed, act_recv = lax.optimization_barrier((summed, act_recv))
    summed = lax.psum_scatter(summed, "z", scatter_dimension=0, tiled=True)
    gradient, row_sums, col_sums = gradient_call(rows, halves, first + second, [act_own, act_recv])

    row_sums = total(reduce_four(row_sums, "x", 4, (1, 2, 3)), "yh", 2)
    row_stats = decay_rate * row_prev + (1.0 - decay_rate) * (row_sums / D)
    scaled = gradient * lax.rsqrt(row_stats)[:, None]
    sums = jnp.concatenate([col_sums, jnp.sum(scaled * scaled, axis=0), row_stats])
    sums = total(total(sums, "core", 2), "yl", 2)
    sums = sums + exchange(sums, "z", 8, 1)
    sums = reduce_four(sums, "z", 8, (2, 4, 6))
    sums, summed = lax.optimization_barrier((sums, summed))
    row_mean = jnp.sum(sums[1536:]) / FF
    col_stats = decay_rate * col_prev + (1.0 - decay_rate) * (sums[:768] / FF)
    part = jnp.sum((sums[768:1536] / col_stats).reshape(6, 128), axis=0)
    part = total(reduce_four(part, "x", 4, (1, 2, 3)), "yh", 2)

    summed = summed.reshape(8, 32, HALF)
    low, high = summed[:, :, :192], summed[:, :, 192:]
    mine = jnp.where(yl == 0, low, high)
    theirs = jnp.where(yl == 0, high, low)
    mine = (mine + exchange(theirs, "yl", 2, 1)).astype(jnp.bfloat16)
    input_grad = mine.reshape(256, 192)
    part, input_grad = lax.optimization_barrier((part, input_grad))

    squares_total = jnp.sum(part) * row_mean
    root_mean = jnp.sqrt(squares_total / (FF * D))
    unclipped = gradient * lax.rsqrt(row_stats[:, None] * col_stats[None, :] / row_mean)
    update = unclipped / jnp.maximum(1.0, root_mean)
    return (input_grad, update)


def solution(mesh):
    fine = Mesh(mesh.devices.reshape(4, 2, 2, 2, 8), ("x", "yh", "yl", "core", "z"))
    row, col = ("x", "yh"), ("yl", "core")
    return jax.shard_map(
        body,
        mesh=fine,
        in_specs=(
            P(("z",) + row, col),
            P("z", row + col),
            P(col + ("z",), row),
            P(col + ("z",)),
            P(row),
        ),
        out_specs=(P("z", row + col), P(col + ("z",), row)),
        check_vma=False,
    )
```

```python
import jax
import jax.numpy as jnp
from jax import lax
from jax.experimental import pallas as pl
from jax.experimental.pallas import tpu as pltpu
from jax.sharding import Mesh
from jax.sharding import PartitionSpec as P

D = 6144
FF = 24576
HALF = 384
FIRST, SECOND = 3, 5
VMEM = 28 * 1024 * 1024

epsilon = 1e-30
decay_rate = 0.9


def exchange(value, axis, size, bit):
    return lax.ppermute(value, axis, [(i, i ^ bit) for i in range(size)])


def shift(value, axis, size, step):
    return lax.ppermute(value, axis, [(i, (i + step) % size) for i in range(size)])


def total(value, axis, size):
    bit = 1
    while bit < size:
        value = value + exchange(value, axis, size, bit)
        bit *= 2
    return value


def reduce_four(value, axis, size, bits):
    others = [exchange(value, axis, size, bit) for bit in bits]
    for other in others:
        value = value + other
    return value


def weight_kernel(core_ref, weight_ref, keep_ref, send_ref):
    weight = weight_ref[...]
    even = jnp.concatenate([weight[:, :192], weight[:, HALF : HALF + 192]], axis=1)
    odd = jnp.concatenate([weight[:, 192:HALF], weight[:, HALF + 192 :]], axis=1)
    first = core_ref[0] == 0
    keep_ref[...] = jnp.where(first, even, odd)
    send_ref[...] = jnp.where(first, odd, even)


def weight_call(halves, weight):
    spec = pl.BlockSpec((256, HALF), lambda s, halves: (s, 0))
    return pl.pallas_call(
        weight_kernel,
        grid_spec=pltpu.PrefetchScalarGridSpec(
            num_scalar_prefetch=1,
            grid=(3,),
            in_specs=[pl.BlockSpec((256, 768), lambda s, halves: (s, 0))],
            out_specs=[spec, spec],
        ),
        out_shape=[jax.ShapeDtypeStruct((768, HALF), jnp.bfloat16)] * 2,
        compiler_params=pltpu.CompilerParams(vmem_limit_bytes=VMEM),
    )(halves, weight)


VECTORS = pl.BlockSpec(memory_space=pltpu.VMEM)
SCALARS = pl.BlockSpec(memory_space=pltpu.SMEM)
PARAMS = pltpu.CompilerParams(vmem_limit_bytes=VMEM)


def tokens(refs):
    return jnp.concatenate([ref[...].reshape(256, 768) for ref in refs], axis=0)


def first_kernel(*refs):
    cot = tokens(refs[:FIRST])
    keep_ref, send_ref, out, *sent = refs[FIRST:]
    kept = jnp.dot(cot, keep_ref[...], preferred_element_type=jnp.float32)
    other = jnp.dot(cot, send_ref[...], preferred_element_type=jnp.float32)
    for j in range(FIRST):
        out[:, j] = kept[j * 256 : (j + 1) * 256].reshape(8, 32, HALF)
        sent[j][...] = other[j * 256 : (j + 1) * 256].reshape(8, 32, HALF)


def second_kernel(rows_ref, *refs):
    cots, others = tokens(refs[:SECOND]), tokens(refs[SECOND : 2 * SECOND])
    keep_ref, other_ref, before_ref, *received, out = refs[2 * SECOND :]
    part = jnp.dot(cots, keep_ref[...], preferred_element_type=jnp.float32) + jnp.dot(
        others, other_ref[...], preferred_element_type=jnp.float32
    )
    for j in range(FIRST):
        out[:, rows_ref[j]] = before_ref[:, j] + received[j][...]
    for j in range(SECOND):
        out[:, rows_ref[FIRST + j]] = part[j * 256 : (j + 1) * 256].reshape(8, 32, HALF)


def first_call(cots, keep, send):
    return pl.pallas_call(
        first_kernel,
        in_specs=[VECTORS] * (FIRST + 2),
        out_specs=[VECTORS] * (1 + FIRST),
        out_shape=[jax.ShapeDtypeStruct((8, FIRST, 32, HALF), jnp.float32)]
        + [jax.ShapeDtypeStruct((8, 32, HALF), jnp.float32)] * FIRST,
        compiler_params=PARAMS,
        cost_estimate=pl.CostEstimate(
            flops=FIRST * 4 * 256 * 768 * HALF, bytes_accessed=4 * 1024 * 1024, transcendentals=0
        ),
    )(*cots, keep, send)


def second_call(rows, cots, others, keep, other_keep, before, received):
    return pl.pallas_call(
        second_kernel,
        in_specs=[SCALARS] + [VECTORS] * (2 * SECOND + 3 + FIRST),
        out_specs=VECTORS,
        out_shape=jax.ShapeDtypeStruct((8, 8, 32, HALF), jnp.float32),
        compiler_params=PARAMS,
        cost_estimate=pl.CostEstimate(
            flops=SECOND * 4 * 256 * 768 * HALF, bytes_accessed=8 * 1024 * 1024, transcendentals=0
        ),
    )(rows, *cots, *others, keep, other_keep, before, *received)


def gradient_kernel(rows_ref, halves_ref, *refs):
    cots, acts, (out_ref, row_ref, col_ref) = refs[:8], refs[8:10], refs[10:]
    act = jnp.concatenate(
        [
            jnp.concatenate([a[:, rows_ref[j]].reshape(256, HALF) for j in range(8)], axis=0)
            for a in acts
        ],
        axis=1,
    )
    whole = lax.dot_general(
        tokens(cots), act, (((0,), (0,)), ((), ())), preferred_element_type=jnp.float32
    )
    for h in range(2):
        columns = pl.ds(pl.multiple_of(halves_ref[h] * HALF, HALF), HALF)
        out_ref[:, columns] = whole[:, h * HALF : (h + 1) * HALF]
    gradient = out_ref[...]
    square = gradient * gradient + epsilon
    col_ref[...] = jnp.sum(square, axis=0)
    lanes = sum(square[:, k * 128 : (k + 1) * 128] for k in range(6))
    row_ref[...] = jnp.sum(lanes.T, axis=0)


def gradient_call(rows, halves, cots, acts):
    return pl.pallas_call(
        gradient_kernel,
        in_specs=[SCALARS] * 2 + [VECTORS] * 10,
        out_specs=[VECTORS] * 3,
        out_shape=[
            jax.ShapeDtypeStruct((768, 768), jnp.float32),
            jax.ShapeDtypeStruct((768,), jnp.float32),
            jax.ShapeDtypeStruct((768,), jnp.float32),
        ],
        compiler_params=PARAMS,
        cost_estimate=pl.CostEstimate(
            flops=2 * 2048 * 768 * 768, bytes_accessed=9 * 1024 * 1024, transcendentals=0
        ),
    )(rows, halves, *cots, *acts)


def body(cotangent, activations, weight, row_prev, col_prev):
    x, yh, core = lax.axis_index("x"), lax.axis_index("yh"), lax.axis_index("core")
    yl = lax.axis_index("yl")

    act_cols = lax.all_gather(activations, ("yl", "core"), axis=1, tiled=True)
    act_half = lax.dynamic_slice_in_dim(act_cols, core * HALF, HALF, 1)
    act_half, cotangent = lax.optimization_barrier((act_half, cotangent))
    act_own = lax.all_gather(act_half, "z", axis=0, tiled=True).reshape(8, 8, 32, HALF)

    own_cot = lax.all_to_all(cotangent, "z", 1, 0, tiled=True).reshape(8, 32, 768)
    own_cot, weight = lax.optimization_barrier((own_cot, weight))
    right, left, far = (x + 3) % 4, (x + 1) % 4, (x + 2) % 4
    columns = [x, x, far, right, left, far, right, left]
    sides = [yh, 1 - yh, yh, yh, yh, 1 - yh, 1 - yh, 1 - yh]
    rows = jnp.stack([c * 2 + side for c, side in zip(columns, sides)]).astype(jnp.int32)
    halves = jnp.stack([core, 1 - core]).astype(jnp.int32)
    keep, send = weight_call(halves, weight)

    other_cot = exchange(own_cot, "yh", 2, 1)
    other_cot, keep, send, rows, halves = lax.optimization_barrier((other_cot, keep, send, rows, halves))
    right_cot = shift(own_cot, "x", 4, 1)
    left_cot = shift(own_cot, "x", 4, -1)
    far_cot = shift(own_cot, "x", 4, 2)
    other_right = shift(other_cot, "x", 4, 1)
    other_left = shift(other_cot, "x", 4, -1)
    other_far = exchange(far_cot, "yh", 2, 1)
    first = [own_cot, other_cot, far_cot]
    second = [right_cot, left_cot, other_far, other_right, other_left]

    kept, *sent = first_call(first, keep, send)
    second[0], second[1], *sent = lax.optimization_barrier((second[0], second[1], *sent))
    received = [exchange(part, "core", 2, 1) for part in sent]
    others = [exchange(cot, "core", 2, 1) for cot in second]
    other_keep = exchange(send, "core", 2, 1)
    *arrived, other_keep, kept, act_own = lax.optimization_barrier(
        (*first, *second, *others, *received, other_keep, kept, act_own)
    )
    first, second, others, received = arrived[:FIRST], arrived[FIRST:8], arrived[8:13], arrived[13:]
    act_recv = exchange(act_own, "core", 2, 1)
    summed = second_call(rows, second, others, keep, other_keep, kept, received)
    summed, act_recv = lax.optimization_barrier((summed, act_recv))
    summed = lax.psum_scatter(summed, "z", scatter_dimension=0, tiled=True)
    gradient, row_sums, col_sums = gradient_call(rows, halves, first + second, [act_own, act_recv])

    row_sums = total(reduce_four(row_sums, "x", 4, (1, 2, 3)), "yh", 2)
    row_stats = decay_rate * row_prev + (1.0 - decay_rate) * (row_sums / D)
    scaled = gradient * lax.rsqrt(row_stats)[:, None]
    sums = jnp.concatenate([col_sums, jnp.sum(scaled * scaled, axis=0), row_stats])
    sums = total(total(sums, "core", 2), "yl", 2)
    sums = sums + exchange(sums, "z", 8, 1)
    sums, summed = lax.optimization_barrier((sums, summed))
    sums = reduce_four(sums, "z", 8, (2, 4, 6))
    row_mean = jnp.sum(sums[1536:]) / FF
    col_stats = decay_rate * col_prev + (1.0 - decay_rate) * (sums[:768] / FF)
    part = jnp.sum((sums[768:1536] / col_stats).reshape(6, 128), axis=0)
    part = total(reduce_four(part, "x", 4, (1, 2, 3)), "yh", 2)

    summed = summed.reshape(8, 32, HALF)
    low, high = summed[:, :, :192], summed[:, :, 192:]
    mine = jnp.where(yl == 0, low, high)
    theirs = jnp.where(yl == 0, high, low)
    mine = (mine + exchange(theirs, "yl", 2, 1)).astype(jnp.bfloat16)
    input_grad = mine.reshape(256, 192)
    part, input_grad = lax.optimization_barrier((part, input_grad))

    squares_total = jnp.sum(part) * row_mean
    root_mean = jnp.sqrt(squares_total / (FF * D))
    unclipped = gradient * lax.rsqrt(row_stats[:, None] * col_stats[None, :] / row_mean)
    update = unclipped / jnp.maximum(1.0, root_mean)
    return (input_grad, update)


def solution(mesh):
    fine = Mesh(mesh.devices.reshape(4, 2, 2, 2, 8), ("x", "yh", "yl", "core", "z"))
    row, col = ("x", "yh"), ("yl", "core")
    return jax.shard_map(
        body,
        mesh=fine,
        in_specs=(
            P(("z",) + row, col),
            P("z", row + col),
            P(col + ("z",), row),
            P(col + ("z",)),
            P(row),
        ),
        out_specs=(P("z", row + col), P(col + ("z",), row)),
        check_vma=False,
    )
```

```python
import jax
import jax.numpy as jnp
from jax import lax
from jax.experimental import pallas as pl
from jax.experimental.pallas import tpu as pltpu
from jax.sharding import Mesh
from jax.sharding import PartitionSpec as P

D = 6144
FF = 24576
HALF = 384
FIRST, SECOND = 3, 5
VMEM = 28 * 1024 * 1024
STEP = 4

epsilon = 1e-30
decay_rate = 0.9


def exchange(value, axis, size, bit):
    return lax.ppermute(value, axis, [(i, i ^ bit) for i in range(size)])


def shift(value, axis, size, step):
    return lax.ppermute(value, axis, [(i, (i + step) % size) for i in range(size)])


def total(value, axis, size):
    bit = 1
    while bit < size:
        value = value + exchange(value, axis, size, bit)
        bit *= 2
    return value


def reduce_four(value, axis, size, bits):
    others = [exchange(value, axis, size, bit) for bit in bits]
    for other in others:
        value = value + other
    return value


def weight_kernel(core_ref, weight_ref, keep_ref, send_ref):
    weight = weight_ref[...]
    even = jnp.concatenate([weight[:, :192], weight[:, HALF : HALF + 192]], axis=1)
    odd = jnp.concatenate([weight[:, 192:HALF], weight[:, HALF + 192 :]], axis=1)
    first = core_ref[0] == 0
    keep_ref[...] = jnp.where(first, even, odd)
    send_ref[...] = jnp.where(first, odd, even)


def weight_call(halves, weight):
    spec = pl.BlockSpec((256, HALF), lambda s, halves: (s, 0))
    return pl.pallas_call(
        weight_kernel,
        grid_spec=pltpu.PrefetchScalarGridSpec(
            num_scalar_prefetch=1,
            grid=(3,),
            in_specs=[pl.BlockSpec((256, 768), lambda s, halves: (s, 0))],
            out_specs=[spec, spec],
        ),
        out_shape=[jax.ShapeDtypeStruct((768, HALF), jnp.bfloat16)] * 2,
        compiler_params=pltpu.CompilerParams(vmem_limit_bytes=60 * 1024 * 1024),
    )(halves, weight)


VECTORS = pl.BlockSpec(memory_space=pltpu.VMEM)
SCALARS = pl.BlockSpec(memory_space=pltpu.SMEM)
PARAMS = pltpu.CompilerParams(vmem_limit_bytes=60 * 1024 * 1024)


def tokens(refs):
    return jnp.concatenate([ref[...].reshape(-1, 768) for ref in refs], axis=0)


def first_kernel(*refs):
    cot = tokens(refs[:FIRST])
    keep_ref, send_ref, out, *sent = refs[FIRST:]
    kept = jnp.dot(cot, keep_ref[...], preferred_element_type=jnp.float32)
    other = jnp.dot(cot, send_ref[...], preferred_element_type=jnp.float32)
    for j in range(FIRST):
        out[:, j] = kept[j * 256 : (j + 1) * 256].reshape(8, 32, HALF)
        sent[j][...] = other[j * 256 : (j + 1) * 256].reshape(8, 32, HALF)


def second_kernel(rows_ref, *refs):
    cots, others = tokens(refs[:SECOND]), tokens(refs[SECOND : 2 * SECOND])
    keep_ref, other_ref, before_ref, *received, out = refs[2 * SECOND :]
    part = jnp.dot(cots, keep_ref[...], preferred_element_type=jnp.float32) + jnp.dot(
        others, other_ref[...], preferred_element_type=jnp.float32
    )
    for j in range(FIRST):
        out[:, rows_ref[j]] = before_ref[:, j] + received[j][...]
    for j in range(SECOND):
        rows = part[j * STEP * 32 : (j + 1) * STEP * 32]
        out[:, rows_ref[FIRST + j]] = rows.reshape(STEP, 32, HALF)


def first_call(cots, keep, send):
    return pl.pallas_call(
        first_kernel,
        in_specs=[VECTORS] * (FIRST + 2),
        out_specs=[VECTORS] * (1 + FIRST),
        out_shape=[jax.ShapeDtypeStruct((8, FIRST, 32, HALF), jnp.float32)]
        + [jax.ShapeDtypeStruct((8, 32, HALF), jnp.float32)] * FIRST,
        compiler_params=PARAMS,
        cost_estimate=pl.CostEstimate(
            flops=FIRST * 4 * 256 * 768 * HALF, bytes_accessed=4 * 1024 * 1024, transcendentals=0
        ),
    )(*cots, keep, send)


def second_call(rows, cots, others, keep, other_keep, before, received):
    def step_spec(*shape):
        return pl.BlockSpec((STEP, *shape), lambda s, rows: (s,) + (0,) * len(shape))

    weight = pl.BlockSpec((768, HALF), lambda s, rows: (0, 0))
    return pl.pallas_call(
        second_kernel,
        grid_spec=pltpu.PrefetchScalarGridSpec(
            num_scalar_prefetch=1,
            grid=(8 // STEP,),
            in_specs=[step_spec(32, 768)] * (2 * SECOND)
            + [weight] * 2
            + [step_spec(FIRST, 32, HALF)]
            + [step_spec(32, HALF)] * FIRST,
            out_specs=step_spec(8, 32, HALF),
        ),
        out_shape=jax.ShapeDtypeStruct((8, 8, 32, HALF), jnp.float32),
        compiler_params=pltpu.CompilerParams(vmem_limit_bytes=60 * 1024 * 1024),
        cost_estimate=pl.CostEstimate(
            flops=SECOND * 4 * 256 * 768 * HALF, bytes_accessed=8 * 1024 * 1024, transcendentals=0
        ),
    )(rows, *cots, *others, keep, other_keep, before, *received)


def gradient_kernel(rows_ref, halves_ref, *refs):
    cots, acts, (out_ref, row_ref, col_ref) = refs[:8], refs[8:10], refs[10:]
    act = jnp.concatenate(
        [
            jnp.concatenate([a[:, rows_ref[j]].reshape(256, HALF) for j in range(8)], axis=0)
            for a in acts
        ],
        axis=1,
    )
    whole = lax.dot_general(
        tokens(cots), act, (((0,), (0,)), ((), ())), preferred_element_type=jnp.float32
    )
    for h in range(2):
        columns = pl.ds(pl.multiple_of(halves_ref[h] * HALF, HALF), HALF)
        out_ref[:, columns] = whole[:, h * HALF : (h + 1) * HALF]
    gradient = out_ref[...]
    square = gradient * gradient + epsilon
    col_ref[...] = jnp.sum(square, axis=0)
    lanes = sum(square[:, k * 128 : (k + 1) * 128] for k in range(6))
    row_ref[...] = jnp.sum(lanes.T, axis=0)


def gradient_call(rows, halves, cots, acts):
    return pl.pallas_call(
        gradient_kernel,
        in_specs=[SCALARS] * 2 + [VECTORS] * 10,
        out_specs=[VECTORS] * 3,
        out_shape=[
            jax.ShapeDtypeStruct((768, 768), jnp.float32),
            jax.ShapeDtypeStruct((768,), jnp.float32),
            jax.ShapeDtypeStruct((768,), jnp.float32),
        ],
        compiler_params=PARAMS,
        cost_estimate=pl.CostEstimate(
            flops=2 * 2048 * 768 * 768, bytes_accessed=9 * 1024 * 1024, transcendentals=0
        ),
    )(rows, halves, *cots, *acts)


def body(cotangent, activations, weight, row_prev, col_prev):
    x, yh, core = lax.axis_index("x"), lax.axis_index("yh"), lax.axis_index("core")
    yl = lax.axis_index("yl")

    act_cols = lax.all_gather(activations, ("yl", "core"), axis=1, tiled=True)
    act_half = lax.dynamic_slice_in_dim(act_cols, core * HALF, HALF, 1)
    act_half, cotangent = lax.optimization_barrier((act_half, cotangent))
    act_own = lax.all_gather(act_half, "z", axis=0, tiled=True).reshape(8, 8, 32, HALF)

    own_cot = lax.all_to_all(cotangent, "z", 1, 0, tiled=True).reshape(8, 32, 768)
    own_cot, weight = lax.optimization_barrier((own_cot, weight))
    right, left, far = (x + 3) % 4, (x + 1) % 4, (x + 2) % 4
    columns = [x, x, far, right, left, far, right, left]
    sides = [yh, 1 - yh, yh, yh, yh, 1 - yh, 1 - yh, 1 - yh]
    rows = jnp.stack([c * 2 + side for c, side in zip(columns, sides)]).astype(jnp.int32)
    halves = jnp.stack([core, 1 - core]).astype(jnp.int32)
    keep, send = weight_call(halves, weight)

    other_cot = exchange(own_cot, "yh", 2, 1)
    other_cot, keep, send, rows, halves = lax.optimization_barrier((other_cot, keep, send, rows, halves))
    right_cot = shift(own_cot, "x", 4, 1)
    left_cot = shift(own_cot, "x", 4, -1)
    far_cot = shift(own_cot, "x", 4, 2)
    other_right = shift(other_cot, "x", 4, 1)
    other_left = shift(other_cot, "x", 4, -1)
    other_far = exchange(far_cot, "yh", 2, 1)
    first = [own_cot, other_cot, far_cot]
    second = [right_cot, left_cot, other_far, other_right, other_left]

    kept, *sent = first_call(first, keep, send)
    second[0], second[1], *sent = lax.optimization_barrier((second[0], second[1], *sent))
    received = [exchange(part, "core", 2, 1) for part in sent]
    others = [exchange(cot, "core", 2, 1) for cot in second]
    other_keep = exchange(send, "core", 2, 1)
    *arrived, other_keep, kept, act_own = lax.optimization_barrier(
        (*first, *second, *others, *received, other_keep, kept, act_own)
    )
    first, second, others, received = arrived[:FIRST], arrived[FIRST:8], arrived[8:13], arrived[13:]
    act_recv = exchange(act_own, "core", 2, 1)
    summed = second_call(rows, second, others, keep, other_keep, kept, received)
    summed, act_recv = lax.optimization_barrier((summed, act_recv))
    summed = lax.psum_scatter(summed, "z", scatter_dimension=0, tiled=True)
    gradient, row_sums, col_sums = gradient_call(rows, halves, first + second, [act_own, act_recv])

    row_sums = total(reduce_four(row_sums, "x", 4, (1, 2, 3)), "yh", 2)
    row_stats = decay_rate * row_prev + (1.0 - decay_rate) * (row_sums / D)
    scaled = gradient * lax.rsqrt(row_stats)[:, None]
    sums = jnp.concatenate([col_sums, jnp.sum(scaled * scaled, axis=0), row_stats])
    sums = total(total(sums, "core", 2), "yl", 2)
    sums = sums + exchange(sums, "z", 8, 1)
    sums = reduce_four(sums, "z", 8, (2, 4, 6))
    row_mean = jnp.sum(sums[1536:]) / FF
    col_stats = decay_rate * col_prev + (1.0 - decay_rate) * (sums[:768] / FF)
    part = jnp.sum((sums[768:1536] / col_stats).reshape(6, 128), axis=0)
    part = reduce_four(part, "x", 4, (1, 2, 3))
    part, summed = lax.optimization_barrier((part, summed))
    part = total(part, "yh", 2)

    summed = summed.reshape(8, 32, HALF)
    low, high = summed[:, :, :192], summed[:, :, 192:]
    mine = jnp.where(yl == 0, low, high)
    theirs = jnp.where(yl == 0, high, low)
    mine = (mine + exchange(theirs, "yl", 2, 1)).astype(jnp.bfloat16)
    input_grad = mine.reshape(256, 192)
    part, input_grad = lax.optimization_barrier((part, input_grad))

    squares_total = jnp.sum(part) * row_mean
    root_mean = jnp.sqrt(squares_total / (FF * D))
    unclipped = gradient * lax.rsqrt(row_stats[:, None] * col_stats[None, :] / row_mean)
    update = unclipped / jnp.maximum(1.0, root_mean)
    return (input_grad, update)


def solution(mesh):
    fine = Mesh(mesh.devices.reshape(4, 2, 2, 2, 8), ("x", "yh", "yl", "core", "z"))
    row, col = ("x", "yh"), ("yl", "core")
    return jax.shard_map(
        body,
        mesh=fine,
        in_specs=(
            P(("z",) + row, col),
            P("z", row + col),
            P(col + ("z",), row),
            P(col + ("z",)),
            P(row),
        ),
        out_specs=(P("z", row + col), P(col + ("z",), row)),
        check_vma=False,
    )
```

```python
import jax
import jax.numpy as jnp
from jax import lax
from jax.experimental.layout import Layout, with_layout_constraint
from jax.experimental import pallas as pl
from jax.experimental.pallas import tpu as pltpu
from jax.sharding import Mesh
from jax.sharding import PartitionSpec as P

D = 6144
FF = 24576
HALF = 384
FIRST, SECOND = 3, 5
VMEM = 28 * 1024 * 1024
STEP = 4

epsilon = 1e-30
decay_rate = 0.9


def exchange(value, axis, size, bit):
    return lax.ppermute(value, axis, [(i, i ^ bit) for i in range(size)])


def shift(value, axis, size, step):
    return lax.ppermute(value, axis, [(i, (i + step) % size) for i in range(size)])


def total(value, axis, size):
    bit = 1
    while bit < size:
        value = value + exchange(value, axis, size, bit)
        bit *= 2
    return value


def reduce_four(value, axis, size, bits):
    others = [exchange(value, axis, size, bit) for bit in bits]
    for other in others:
        value = value + other
    return value


def weight_kernel(core_ref, weight_ref, keep_ref, send_ref):
    weight = weight_ref[...]
    even = jnp.concatenate([weight[:, :192], weight[:, HALF : HALF + 192]], axis=1)
    odd = jnp.concatenate([weight[:, 192:HALF], weight[:, HALF + 192 :]], axis=1)
    first = core_ref[0] == 0
    keep_ref[...] = jnp.where(first, even, odd)
    send_ref[...] = jnp.where(first, odd, even)


def weight_call(halves, weight):
    spec = pl.BlockSpec((256, HALF), lambda s, halves: (s, 0))
    return pl.pallas_call(
        weight_kernel,
        grid_spec=pltpu.PrefetchScalarGridSpec(
            num_scalar_prefetch=1,
            grid=(3,),
            in_specs=[pl.BlockSpec((256, 768), lambda s, halves: (s, 0))],
            out_specs=[spec, spec],
        ),
        out_shape=[jax.ShapeDtypeStruct((768, HALF), jnp.bfloat16)] * 2,
        compiler_params=pltpu.CompilerParams(vmem_limit_bytes=60 * 1024 * 1024),
    )(halves, weight)


VECTORS = pl.BlockSpec(memory_space=pltpu.VMEM)
SCALARS = pl.BlockSpec(memory_space=pltpu.SMEM)
PARAMS = pltpu.CompilerParams(vmem_limit_bytes=60 * 1024 * 1024)


def tokens(refs):
    return jnp.concatenate([ref[...].reshape(-1, 768) for ref in refs], axis=0)


def first_kernel(*refs):
    cot = tokens(refs[:FIRST])
    keep_ref, send_ref, out, *sent = refs[FIRST:]
    kept = jnp.dot(cot, keep_ref[...], preferred_element_type=jnp.float32)
    other = jnp.dot(cot, send_ref[...], preferred_element_type=jnp.float32)
    for j in range(FIRST):
        out[:, j] = kept[j * 256 : (j + 1) * 256].reshape(8, 32, HALF)
        sent[j][...] = other[j * 256 : (j + 1) * 256].reshape(8, 32, HALF)


def second_kernel(rows_ref, *refs):
    cots, others = tokens(refs[:SECOND]), tokens(refs[SECOND : 2 * SECOND])
    keep_ref, other_ref, before_ref, *received, out = refs[2 * SECOND :]
    part = jnp.dot(cots, keep_ref[...], preferred_element_type=jnp.float32) + jnp.dot(
        others, other_ref[...], preferred_element_type=jnp.float32
    )
    for j in range(FIRST):
        out[:, rows_ref[j]] = before_ref[:, j] + received[j][...]
    for j in range(SECOND):
        rows = part[j * STEP * 32 : (j + 1) * STEP * 32]
        out[:, rows_ref[FIRST + j]] = rows.reshape(STEP, 32, HALF)


def first_call(cots, keep, send):
    return pl.pallas_call(
        first_kernel,
        in_specs=[VECTORS] * (FIRST + 2),
        out_specs=[VECTORS] * (1 + FIRST),
        out_shape=[jax.ShapeDtypeStruct((8, FIRST, 32, HALF), jnp.float32)]
        + [jax.ShapeDtypeStruct((8, 32, HALF), jnp.float32)] * FIRST,
        compiler_params=PARAMS,
        cost_estimate=pl.CostEstimate(
            flops=FIRST * 4 * 256 * 768 * HALF, bytes_accessed=4 * 1024 * 1024, transcendentals=0
        ),
    )(*cots, keep, send)


def second_call(rows, cots, others, keep, other_keep, before, received):
    def step_spec(*shape):
        return pl.BlockSpec((STEP, *shape), lambda s, rows: (s,) + (0,) * len(shape))

    weight = pl.BlockSpec((768, HALF), lambda s, rows: (0, 0))
    return pl.pallas_call(
        second_kernel,
        grid_spec=pltpu.PrefetchScalarGridSpec(
            num_scalar_prefetch=1,
            grid=(8 // STEP,),
            in_specs=[step_spec(32, 768)] * (2 * SECOND)
            + [weight] * 2
            + [step_spec(FIRST, 32, HALF)]
            + [step_spec(32, HALF)] * FIRST,
            out_specs=step_spec(8, 32, HALF),
        ),
        out_shape=jax.ShapeDtypeStruct((8, 8, 32, HALF), jnp.float32),
        compiler_params=pltpu.CompilerParams(vmem_limit_bytes=60 * 1024 * 1024),
        cost_estimate=pl.CostEstimate(
            flops=SECOND * 4 * 256 * 768 * HALF, bytes_accessed=8 * 1024 * 1024, transcendentals=0
        ),
    )(rows, *cots, *others, keep, other_keep, before, *received)


def gradient_kernel(rows_ref, halves_ref, *refs):
    cots, acts, (out_ref, row_ref, col_ref) = refs[:8], refs[8:10], refs[10:]
    act = jnp.concatenate(
        [
            jnp.concatenate([a[:, rows_ref[j]].reshape(256, HALF) for j in range(8)], axis=0)
            for a in acts
        ],
        axis=1,
    )
    whole = lax.dot_general(
        tokens(cots), act, (((0,), (0,)), ((), ())), preferred_element_type=jnp.float32
    )
    for h in range(2):
        columns = pl.ds(pl.multiple_of(halves_ref[h] * HALF, HALF), HALF)
        out_ref[:, columns] = whole[:, h * HALF : (h + 1) * HALF]
    gradient = out_ref[...]
    square = gradient * gradient + epsilon
    col_ref[...] = jnp.sum(square, axis=0)
    lanes = sum(square[:, k * 128 : (k + 1) * 128] for k in range(6))
    row_ref[...] = jnp.sum(lanes.T, axis=0)


def gradient_call(rows, halves, cots, acts):
    return pl.pallas_call(
        gradient_kernel,
        in_specs=[SCALARS] * 2 + [VECTORS] * 10,
        out_specs=[VECTORS] * 3,
        out_shape=[
            jax.ShapeDtypeStruct((768, 768), jnp.float32),
            jax.ShapeDtypeStruct((768,), jnp.float32),
            jax.ShapeDtypeStruct((768,), jnp.float32),
        ],
        compiler_params=PARAMS,
        cost_estimate=pl.CostEstimate(
            flops=2 * 2048 * 768 * 768, bytes_accessed=9 * 1024 * 1024, transcendentals=0
        ),
    )(rows, halves, *cots, *acts)


def body(cotangent, activations, weight, row_prev, col_prev):
    x, yh, core = lax.axis_index("x"), lax.axis_index("yh"), lax.axis_index("core")
    yl = lax.axis_index("yl")

    near = lax.ppermute(activations, ("yl", "core"), [(0, 2), (3, 1), (1, 0), (2, 3)])
    cross = lax.ppermute(activations, ("yl", "core"), [(1, 2), (2, 1)])
    same = jnp.where(yl == core, activations, near)
    opposite = jnp.where(yl == core, near, cross)
    act_half = jnp.where(
        core == 0,
        jnp.concatenate([same, opposite], axis=1),
        jnp.concatenate([opposite, same], axis=1),
    )
    act_half = with_layout_constraint(act_half, Layout((0, 1)))
    act_half, cotangent = lax.optimization_barrier((act_half, cotangent))
    act_own = lax.all_gather(act_half, "z", axis=0, tiled=True)
    act_own = with_layout_constraint(act_own, Layout((0, 1))).reshape(8, 8, 32, HALF)

    own_cot = lax.all_to_all(cotangent, "z", 1, 0, tiled=True).reshape(8, 32, 768)
    own_cot, weight = lax.optimization_barrier((own_cot, weight))
    right, left, far = (x + 3) % 4, (x + 1) % 4, (x + 2) % 4
    columns = [x, x, far, right, left, far, right, left]
    sides = [yh, 1 - yh, yh, yh, yh, 1 - yh, 1 - yh, 1 - yh]
    rows = jnp.stack([c * 2 + side for c, side in zip(columns, sides)]).astype(jnp.int32)
    halves = jnp.stack([core, 1 - core]).astype(jnp.int32)
    keep, send = weight_call(halves, weight)

    other_cot = exchange(own_cot, "yh", 2, 1)
    other_cot, keep, send, rows, halves = lax.optimization_barrier((other_cot, keep, send, rows, halves))
    right_cot = shift(own_cot, "x", 4, 1)
    left_cot = shift(own_cot, "x", 4, -1)
    far_cot = shift(own_cot, "x", 4, 2)
    other_right = shift(other_cot, "x", 4, 1)
    other_left = shift(other_cot, "x", 4, -1)
    other_far = exchange(far_cot, "yh", 2, 1)
    first = [own_cot, other_cot, far_cot]
    second = [right_cot, left_cot, other_far, other_right, other_left]

    kept, *sent = first_call(first, keep, send)
    second[0], second[1], *sent = lax.optimization_barrier((second[0], second[1], *sent))
    received = [exchange(part, "core", 2, 1) for part in sent]
    others = [exchange(cot, "core", 2, 1) for cot in second]
    other_keep = exchange(send, "core", 2, 1)
    *arrived, other_keep, kept, act_own = lax.optimization_barrier(
        (*first, *second, *others, *received, other_keep, kept, act_own)
    )
    first, second, others, received = arrived[:FIRST], arrived[FIRST:8], arrived[8:13], arrived[13:]
    act_recv = exchange(act_own, "core", 2, 1)
    summed = second_call(rows, second, others, keep, other_keep, kept, received)
    summed, act_recv = lax.optimization_barrier((summed, act_recv))
    summed = lax.psum_scatter(summed, "z", scatter_dimension=0, tiled=True)
    gradient, row_sums, col_sums = gradient_call(rows, halves, first + second, [act_own, act_recv])

    row_sums = total(reduce_four(row_sums, "x", 4, (1, 2, 3)), "yh", 2)
    row_stats = decay_rate * row_prev + (1.0 - decay_rate) * (row_sums / D)
    scaled = gradient * lax.rsqrt(row_stats)[:, None]
    sums = jnp.concatenate([col_sums, jnp.sum(scaled * scaled, axis=0), row_stats])
    sums = total(total(sums, "core", 2), "yl", 2)
    sums = sums + exchange(sums, "z", 8, 1)
    sums = reduce_four(sums, "z", 8, (2, 4, 6))
    row_mean = jnp.sum(sums[1536:]) / FF
    col_stats = decay_rate * col_prev + (1.0 - decay_rate) * (sums[:768] / FF)
    part = jnp.sum((sums[768:1536] / col_stats).reshape(6, 128), axis=0)
    others = [exchange(part, "x", 4, bit) for bit in (1, 2, 3)]
    part = part + others[0]
    part, summed = lax.optimization_barrier((part, summed))
    part = total(part + others[1] + others[2], "yh", 2)

    summed = summed.reshape(8, 32, HALF)
    low, high = summed[:, :, :192], summed[:, :, 192:]
    mine = jnp.where(yl == 0, low, high)
    theirs = jnp.where(yl == 0, high, low)
    mine = (mine + exchange(theirs, "yl", 2, 1)).astype(jnp.bfloat16)
    input_grad = mine.reshape(256, 192)
    part, input_grad = lax.optimization_barrier((part, input_grad))

    squares_total = jnp.sum(part) * row_mean
    root_mean = jnp.sqrt(squares_total / (FF * D))
    unclipped = gradient * lax.rsqrt(row_stats[:, None] * col_stats[None, :] / row_mean)
    update = unclipped / jnp.maximum(1.0, root_mean)
    return (input_grad, update)


def solution(mesh):
    fine = Mesh(mesh.devices.reshape(4, 2, 2, 2, 8), ("x", "yh", "yl", "core", "z"))
    row, col = ("x", "yh"), ("yl", "core")
    return jax.shard_map(
        body,
        mesh=fine,
        in_specs=(
            P(("z",) + row, col),
            P("z", row + col),
            P(col + ("z",), row),
            P(col + ("z",)),
            P(row),
        ),
        out_specs=(P("z", row + col), P(col + ("z",), row)),
        check_vma=False,
    )
```

```python
import jax
import jax.numpy as jnp
from jax import lax
from jax.experimental.layout import Layout, with_layout_constraint
from jax.experimental import pallas as pl
from jax.experimental.pallas import tpu as pltpu
from jax.sharding import Mesh
from jax.sharding import PartitionSpec as P

D = 6144
FF = 24576
HALF = 384
FIRST, SECOND = 3, 5
VMEM = 28 * 1024 * 1024
STEP = 4

epsilon = 1e-30
decay_rate = 0.9


def exchange(value, axis, size, bit):
    return lax.ppermute(value, axis, [(i, i ^ bit) for i in range(size)])


def shift(value, axis, size, step):
    return lax.ppermute(value, axis, [(i, (i + step) % size) for i in range(size)])


def total(value, axis, size):
    bit = 1
    while bit < size:
        value = value + exchange(value, axis, size, bit)
        bit *= 2
    return value


def reduce_four(value, axis, size, bits):
    others = [exchange(value, axis, size, bit) for bit in bits]
    for other in others:
        value = value + other
    return value


def weight_kernel(core_ref, weight_ref, other_ref, keep_ref, send_ref, other_keep_ref):
    def columns(weight, odd):
        start = 192 if odd else 0
        return jnp.concatenate([weight[:, start : start + 192], weight[:, HALF + start : HALF + start + 192]], axis=1)

    weight, other = weight_ref[...], other_ref[...]
    first = core_ref[0] == 0
    even, odd = columns(weight, False), columns(weight, True)
    keep_ref[...] = jnp.where(first, even, odd)
    send_ref[...] = jnp.where(first, odd, even)
    other_keep_ref[...] = jnp.where(first, columns(other, False), columns(other, True))


def weight_call(halves, weight, other):
    whole = pl.BlockSpec((256, 768), lambda s, halves: (s, 0))
    half = pl.BlockSpec((256, HALF), lambda s, halves: (s, 0))
    return pl.pallas_call(
        weight_kernel,
        grid_spec=pltpu.PrefetchScalarGridSpec(
            num_scalar_prefetch=1,
            grid=(3,),
            in_specs=[whole, whole],
            out_specs=[half] * 3,
        ),
        out_shape=[jax.ShapeDtypeStruct((768, HALF), jnp.bfloat16)] * 3,
        compiler_params=pltpu.CompilerParams(vmem_limit_bytes=60 * 1024 * 1024),
    )(halves, weight, other)


VECTORS = pl.BlockSpec(memory_space=pltpu.VMEM)
SCALARS = pl.BlockSpec(memory_space=pltpu.SMEM)
PARAMS = pltpu.CompilerParams(vmem_limit_bytes=60 * 1024 * 1024)


def tokens(refs):
    return jnp.concatenate([ref[...].reshape(-1, 768) for ref in refs], axis=0)


def first_kernel(*refs):
    cot = tokens(refs[:FIRST])
    keep_ref, send_ref, out, *sent = refs[FIRST:]
    kept = jnp.dot(cot, keep_ref[...], preferred_element_type=jnp.float32)
    other = jnp.dot(cot, send_ref[...], preferred_element_type=jnp.float32)
    for j in range(FIRST):
        out[:, j] = kept[j * 256 : (j + 1) * 256].reshape(8, 32, HALF)
        sent[j][...] = other[j * 256 : (j + 1) * 256].reshape(8, 32, HALF)


def second_kernel(rows_ref, *refs):
    cots, others = tokens(refs[:SECOND]), tokens(refs[SECOND : 2 * SECOND])
    keep_ref, other_ref, before_ref, *received, out = refs[2 * SECOND :]
    part = jnp.dot(cots, keep_ref[...], preferred_element_type=jnp.float32) + jnp.dot(
        others, other_ref[...], preferred_element_type=jnp.float32
    )
    for j in range(FIRST):
        out[:, rows_ref[j]] = before_ref[:, j] + received[j][...]
    for j in range(SECOND):
        rows = part[j * STEP * 32 : (j + 1) * STEP * 32]
        out[:, rows_ref[FIRST + j]] = rows.reshape(STEP, 32, HALF)


def first_call(cots, keep, send):
    return pl.pallas_call(
        first_kernel,
        in_specs=[VECTORS] * (FIRST + 2),
        out_specs=[VECTORS] * (1 + FIRST),
        out_shape=[jax.ShapeDtypeStruct((8, FIRST, 32, HALF), jnp.float32)]
        + [jax.ShapeDtypeStruct((8, 32, HALF), jnp.float32)] * FIRST,
        compiler_params=PARAMS,
        cost_estimate=pl.CostEstimate(
            flops=FIRST * 4 * 256 * 768 * HALF, bytes_accessed=4 * 1024 * 1024, transcendentals=0
        ),
    )(*cots, keep, send)


def second_call(rows, cots, others, keep, other_keep, before, received):
    def step_spec(*shape):
        return pl.BlockSpec((STEP, *shape), lambda s, rows: (s,) + (0,) * len(shape))

    weight = pl.BlockSpec((768, HALF), lambda s, rows: (0, 0))
    return pl.pallas_call(
        second_kernel,
        grid_spec=pltpu.PrefetchScalarGridSpec(
            num_scalar_prefetch=1,
            grid=(8 // STEP,),
            in_specs=[step_spec(32, 768)] * (2 * SECOND)
            + [weight] * 2
            + [step_spec(FIRST, 32, HALF)]
            + [step_spec(32, HALF)] * FIRST,
            out_specs=step_spec(8, 32, HALF),
        ),
        out_shape=jax.ShapeDtypeStruct((8, 8, 32, HALF), jnp.float32),
        compiler_params=pltpu.CompilerParams(vmem_limit_bytes=60 * 1024 * 1024),
        cost_estimate=pl.CostEstimate(
            flops=SECOND * 4 * 256 * 768 * HALF, bytes_accessed=8 * 1024 * 1024, transcendentals=0
        ),
    )(rows, *cots, *others, keep, other_keep, before, *received)


def gradient_kernel(rows_ref, halves_ref, *refs):
    cots, acts, (out_ref, row_ref, col_ref) = refs[:8], refs[8:10], refs[10:]
    act = jnp.concatenate(
        [
            jnp.concatenate([a[:, rows_ref[j]].reshape(256, HALF) for j in range(8)], axis=0)
            for a in acts
        ],
        axis=1,
    )
    whole = lax.dot_general(
        tokens(cots), act, (((0,), (0,)), ((), ())), preferred_element_type=jnp.float32
    )
    for h in range(2):
        columns = pl.ds(pl.multiple_of(halves_ref[h] * HALF, HALF), HALF)
        out_ref[:, columns] = whole[:, h * HALF : (h + 1) * HALF]
    gradient = out_ref[...]
    square = gradient * gradient + epsilon
    col_ref[...] = jnp.sum(square, axis=0)
    lanes = sum(square[:, k * 128 : (k + 1) * 128] for k in range(6))
    row_ref[...] = jnp.sum(lanes.T, axis=0)


def gradient_call(rows, halves, cots, acts):
    return pl.pallas_call(
        gradient_kernel,
        in_specs=[SCALARS] * 2 + [VECTORS] * 10,
        out_specs=[VECTORS] * 3,
        out_shape=[
            jax.ShapeDtypeStruct((768, 768), jnp.float32),
            jax.ShapeDtypeStruct((768,), jnp.float32),
            jax.ShapeDtypeStruct((768,), jnp.float32),
        ],
        compiler_params=PARAMS,
        cost_estimate=pl.CostEstimate(
            flops=2 * 2048 * 768 * 768, bytes_accessed=9 * 1024 * 1024, transcendentals=0
        ),
    )(rows, halves, *cots, *acts)


def body(cotangent, activations, weight, row_prev, col_prev):
    x, yh, core = lax.axis_index("x"), lax.axis_index("yh"), lax.axis_index("core")
    yl = lax.axis_index("yl")

    near = lax.ppermute(activations, ("yl", "core"), [(0, 2), (3, 1), (1, 0), (2, 3)])
    cross = lax.ppermute(activations, ("yl", "core"), [(1, 2), (2, 1)])
    same = jnp.where(yl == core, activations, near)
    opposite = jnp.where(yl == core, near, cross)
    act_half = jnp.where(
        core == 0,
        jnp.concatenate([same, opposite], axis=1),
        jnp.concatenate([opposite, same], axis=1),
    )
    act_half = with_layout_constraint(act_half, Layout((0, 1)))
    act_half, cotangent = lax.optimization_barrier((act_half, cotangent))
    other_weight = exchange(weight, "core", 2, 1)
    act_own = lax.all_gather(act_half, "z", axis=0, tiled=True)
    act_own = with_layout_constraint(act_own, Layout((0, 1))).reshape(8, 8, 32, HALF)

    own_cot = lax.all_to_all(cotangent, "z", 1, 0, tiled=True).reshape(8, 32, 768)
    own_cot, weight, other_weight = lax.optimization_barrier((own_cot, weight, other_weight))
    right, left, far = (x + 3) % 4, (x + 1) % 4, (x + 2) % 4
    columns = [x, x, far, right, left, far, right, left]
    sides = [yh, 1 - yh, yh, yh, yh, 1 - yh, 1 - yh, 1 - yh]
    rows = jnp.stack([c * 2 + side for c, side in zip(columns, sides)]).astype(jnp.int32)
    halves = jnp.stack([core, 1 - core]).astype(jnp.int32)
    keep, send, other_keep = weight_call(halves, weight, other_weight)

    other_cot = exchange(own_cot, "yh", 2, 1)
    other_cot, keep, send, other_keep, rows, halves = lax.optimization_barrier(
        (other_cot, keep, send, other_keep, rows, halves)
    )
    right_cot = shift(own_cot, "x", 4, 1)
    left_cot = shift(own_cot, "x", 4, -1)
    far_cot = shift(own_cot, "x", 4, 2)
    other_right = shift(other_cot, "x", 4, 1)
    other_left = shift(other_cot, "x", 4, -1)
    other_far = exchange(far_cot, "yh", 2, 1)
    first = [own_cot, other_cot, far_cot]
    second = [right_cot, left_cot, other_far, other_right, other_left]

    kept, *sent = first_call(first, keep, send)
    second[0], second[1], *sent = lax.optimization_barrier((second[0], second[1], *sent))
    received = [exchange(part, "core", 2, 1) for part in sent]
    others = [exchange(cot, "core", 2, 1) for cot in second]
    *arrived, kept, act_own = lax.optimization_barrier(
        (*first, *second, *others, *received, kept, act_own)
    )
    first, second, others, received = arrived[:FIRST], arrived[FIRST:8], arrived[8:13], arrived[13:]
    act_recv = exchange(act_own, "core", 2, 1)
    summed = second_call(rows, second, others, keep, other_keep, kept, received)
    summed, act_recv = lax.optimization_barrier((summed, act_recv))
    summed = lax.psum_scatter(summed, "z", scatter_dimension=0, tiled=True)
    gradient, row_sums, col_sums = gradient_call(rows, halves, first + second, [act_own, act_recv])

    row_sums = total(reduce_four(row_sums, "x", 4, (1, 2, 3)), "yh", 2)
    row_stats = decay_rate * row_prev + (1.0 - decay_rate) * (row_sums / D)
    scaled = gradient * lax.rsqrt(row_stats)[:, None]
    sums = jnp.concatenate([col_sums, jnp.sum(scaled * scaled, axis=0), row_stats])
    sums = total(total(sums, "core", 2), "yl", 2)
    sums = sums + exchange(sums, "z", 8, 1)
    sums = reduce_four(sums, "z", 8, (2, 4, 6))
    row_mean = jnp.sum(sums[1536:]) / FF
    col_stats = decay_rate * col_prev + (1.0 - decay_rate) * (sums[:768] / FF)
    part = jnp.sum((sums[768:1536] / col_stats).reshape(6, 128), axis=0)
    others = [exchange(part, "x", 4, bit) for bit in (1, 2, 3)]
    part = part + others[0]
    part, summed = lax.optimization_barrier((part, summed))
    part = part + others[1] + others[2]
    last = exchange(part, "yh", 2, 1)

    summed = summed.reshape(8, 32, HALF)
    low, high = summed[:, :, :192], summed[:, :, 192:]
    mine = jnp.where(yl == 0, low, high)
    theirs = jnp.where(yl == 0, high, low)
    mine = (mine + exchange(theirs, "yl", 2, 1)).astype(jnp.bfloat16)
    input_grad = mine.reshape(256, 192)
    last, input_grad = lax.optimization_barrier((last, input_grad))

    squares_total = jnp.sum(part + last) * row_mean
    root_mean = jnp.sqrt(squares_total / (FF * D))
    unclipped = gradient * lax.rsqrt(row_stats[:, None] * col_stats[None, :] / row_mean)
    update = unclipped / jnp.maximum(1.0, root_mean)
    return (input_grad, update)


def solution(mesh):
    fine = Mesh(mesh.devices.reshape(4, 2, 2, 2, 8), ("x", "yh", "yl", "core", "z"))
    row, col = ("x", "yh"), ("yl", "core")
    return jax.shard_map(
        body,
        mesh=fine,
        in_specs=(
            P(("z",) + row, col),
            P("z", row + col),
            P(col + ("z",), row),
            P(col + ("z",)),
            P(row),
        ),
        out_specs=(P("z", row + col), P(col + ("z",), row)),
        check_vma=False,
    )
```

```python
import jax
import jax.numpy as jnp
from jax import lax
from jax.experimental.layout import Layout, with_layout_constraint
from jax.experimental import pallas as pl
from jax.experimental.pallas import tpu as pltpu
from jax.sharding import Mesh
from jax.sharding import PartitionSpec as P

D = 6144
FF = 24576
HALF = 384
FIRST, SECOND = 3, 5
VMEM = 28 * 1024 * 1024
STEP = 4

epsilon = 1e-30
decay_rate = 0.9


def exchange(value, axis, size, bit):
    return lax.ppermute(value, axis, [(i, i ^ bit) for i in range(size)])


def shift(value, axis, size, step):
    return lax.ppermute(value, axis, [(i, (i + step) % size) for i in range(size)])


def total(value, axis, size):
    bit = 1
    while bit < size:
        value = value + exchange(value, axis, size, bit)
        bit *= 2
    return value


def reduce_four(value, axis, size, bits):
    others = [exchange(value, axis, size, bit) for bit in bits]
    for other in others:
        value = value + other
    return value


def weight_kernel(core_ref, weight_ref, keep_ref, send_ref):
    weight = weight_ref[...]
    even = jnp.concatenate([weight[:, :192], weight[:, HALF : HALF + 192]], axis=1)
    odd = jnp.concatenate([weight[:, 192:HALF], weight[:, HALF + 192 :]], axis=1)
    first = core_ref[0] == 0
    keep_ref[...] = jnp.where(first, even, odd)
    send_ref[...] = jnp.where(first, odd, even)


def weight_call(halves, weight):
    spec = pl.BlockSpec((256, HALF), lambda s, halves: (s, 0))
    return pl.pallas_call(
        weight_kernel,
        grid_spec=pltpu.PrefetchScalarGridSpec(
            num_scalar_prefetch=1,
            grid=(3,),
            in_specs=[pl.BlockSpec((256, 768), lambda s, halves: (s, 0))],
            out_specs=[spec, spec],
        ),
        out_shape=[jax.ShapeDtypeStruct((768, HALF), jnp.bfloat16)] * 2,
        compiler_params=pltpu.CompilerParams(vmem_limit_bytes=60 * 1024 * 1024),
    )(halves, weight)


VECTORS = pl.BlockSpec(memory_space=pltpu.VMEM)
SCALARS = pl.BlockSpec(memory_space=pltpu.SMEM)
PARAMS = pltpu.CompilerParams(vmem_limit_bytes=60 * 1024 * 1024)


def tokens(refs):
    return jnp.concatenate([ref[...].reshape(-1, 768) for ref in refs], axis=0)


def first_kernel(*refs):
    cot = tokens(refs[:FIRST])
    keep_ref, send_ref, out, *sent = refs[FIRST:]
    kept = jnp.dot(cot, keep_ref[...], preferred_element_type=jnp.float32)
    other = jnp.dot(cot, send_ref[...], preferred_element_type=jnp.float32)
    for j in range(FIRST):
        out[:, j] = kept[j * 256 : (j + 1) * 256].reshape(8, 32, HALF)
        sent[j][...] = other[j * 256 : (j + 1) * 256].reshape(8, 32, HALF)


def second_kernel(rows_ref, *refs):
    cots, others = tokens(refs[:SECOND]), tokens(refs[SECOND : 2 * SECOND])
    keep_ref, other_ref, before_ref, *received, out = refs[2 * SECOND :]
    part = jnp.dot(cots, keep_ref[...], preferred_element_type=jnp.float32) + jnp.dot(
        others, other_ref[...], preferred_element_type=jnp.float32
    )
    for j in range(FIRST):
        out[:, rows_ref[j]] = before_ref[:, j] + received[j][...]
    for j in range(SECOND):
        rows = part[j * STEP * 32 : (j + 1) * STEP * 32]
        out[:, rows_ref[FIRST + j]] = rows.reshape(STEP, 32, HALF)


def first_call(cots, keep, send):
    return pl.pallas_call(
        first_kernel,
        in_specs=[VECTORS] * (FIRST + 2),
        out_specs=[VECTORS] * (1 + FIRST),
        out_shape=[jax.ShapeDtypeStruct((8, FIRST, 32, HALF), jnp.float32)]
        + [jax.ShapeDtypeStruct((8, 32, HALF), jnp.float32)] * FIRST,
        compiler_params=PARAMS,
        cost_estimate=pl.CostEstimate(
            flops=FIRST * 4 * 256 * 768 * HALF, bytes_accessed=4 * 1024 * 1024, transcendentals=0
        ),
    )(*cots, keep, send)


def second_call(rows, cots, others, keep, other_keep, before, received):
    def step_spec(*shape):
        return pl.BlockSpec((STEP, *shape), lambda s, rows: (s,) + (0,) * len(shape))

    weight = pl.BlockSpec((768, HALF), lambda s, rows: (0, 0))
    return pl.pallas_call(
        second_kernel,
        grid_spec=pltpu.PrefetchScalarGridSpec(
            num_scalar_prefetch=1,
            grid=(8 // STEP,),
            in_specs=[step_spec(32, 768)] * (2 * SECOND)
            + [weight] * 2
            + [step_spec(FIRST, 32, HALF)]
            + [step_spec(32, HALF)] * FIRST,
            out_specs=step_spec(8, 32, HALF),
        ),
        out_shape=jax.ShapeDtypeStruct((8, 8, 32, HALF), jnp.float32),
        compiler_params=pltpu.CompilerParams(vmem_limit_bytes=60 * 1024 * 1024),
        cost_estimate=pl.CostEstimate(
            flops=SECOND * 4 * 256 * 768 * HALF, bytes_accessed=8 * 1024 * 1024, transcendentals=0
        ),
    )(rows, *cots, *others, keep, other_keep, before, *received)


def gradient_kernel(rows_ref, halves_ref, *refs):
    cots, acts, (out_ref, row_ref, col_ref) = refs[:8], refs[8:10], refs[10:]
    act = jnp.concatenate(
        [
            jnp.concatenate([a[:, rows_ref[j]].reshape(256, HALF) for j in range(8)], axis=0)
            for a in acts
        ],
        axis=1,
    )
    whole = lax.dot_general(
        tokens(cots), act, (((0,), (0,)), ((), ())), preferred_element_type=jnp.float32
    )
    for h in range(2):
        columns = pl.ds(pl.multiple_of(halves_ref[h] * HALF, HALF), HALF)
        out_ref[:, columns] = whole[:, h * HALF : (h + 1) * HALF]
    gradient = out_ref[...]
    square = gradient * gradient + epsilon
    col_ref[...] = jnp.sum(square, axis=0)
    lanes = sum(square[:, k * 128 : (k + 1) * 128] for k in range(6))
    row_ref[...] = jnp.sum(lanes.T, axis=0)


def gradient_call(rows, halves, cots, acts):
    return pl.pallas_call(
        gradient_kernel,
        in_specs=[SCALARS] * 2 + [VECTORS] * 10,
        out_specs=[VECTORS] * 3,
        out_shape=[
            jax.ShapeDtypeStruct((768, 768), jnp.float32),
            jax.ShapeDtypeStruct((768,), jnp.float32),
            jax.ShapeDtypeStruct((768,), jnp.float32),
        ],
        compiler_params=PARAMS,
        cost_estimate=pl.CostEstimate(
            flops=2 * 2048 * 768 * 768, bytes_accessed=9 * 1024 * 1024, transcendentals=0
        ),
    )(rows, halves, *cots, *acts)


def body(cotangent, activations, weight, row_prev, col_prev):
    x, yh, core = lax.axis_index("x"), lax.axis_index("yh"), lax.axis_index("core")
    yl = lax.axis_index("yl")

    near = lax.ppermute(activations, ("yl", "core"), [(0, 2), (3, 1), (1, 0), (2, 3)])
    cross = lax.ppermute(activations, ("yl", "core"), [(1, 2), (2, 1)])
    same = jnp.where(yl == core, activations, near)
    opposite = jnp.where(yl == core, near, cross)
    act_half = jnp.where(
        core == 0,
        jnp.concatenate([same, opposite], axis=1),
        jnp.concatenate([opposite, same], axis=1),
    )
    act_half = with_layout_constraint(act_half, Layout((0, 1)))
    blocks = cotangent.reshape(32, 8, 768).transpose(1, 0, 2)
    act_half, blocks, weight = lax.optimization_barrier((act_half, blocks, weight))
    act_own = lax.all_gather(act_half, "z", axis=0, tiled=True)
    act_own = with_layout_constraint(act_own, Layout((0, 1))).reshape(8, 8, 32, HALF)

    own_cot = lax.all_to_all(blocks, "z", 0, 0, tiled=True)
    right, left, far = (x + 3) % 4, (x + 1) % 4, (x + 2) % 4
    columns = [x, x, far, right, left, far, right, left]
    sides = [yh, 1 - yh, yh, yh, yh, 1 - yh, 1 - yh, 1 - yh]
    rows = jnp.stack([c * 2 + side for c, side in zip(columns, sides)]).astype(jnp.int32)
    halves = jnp.stack([core, 1 - core]).astype(jnp.int32)
    keep, send = weight_call(halves, weight)

    other_keep = exchange(send, "core", 2, 1)
    own_cot, keep, send, other_keep, rows, halves = lax.optimization_barrier(
        (own_cot, keep, send, other_keep, rows, halves)
    )
    other_cot = exchange(own_cot, "yh", 2, 1)
    right_cot = shift(own_cot, "x", 4, 1)
    left_cot = shift(own_cot, "x", 4, -1)
    far_cot = shift(own_cot, "x", 4, 2)
    other_right = shift(other_cot, "x", 4, 1)
    other_left = shift(other_cot, "x", 4, -1)
    other_far = exchange(far_cot, "yh", 2, 1)
    first = [own_cot, other_cot, far_cot]
    second = [right_cot, left_cot, other_far, other_right, other_left]

    kept, *sent = first_call(first, keep, send)
    second[0], second[1], second[2], *sent = lax.optimization_barrier(
        (second[0], second[1], second[2], *sent)
    )
    received = [exchange(part, "core", 2, 1) for part in sent]
    others = [exchange(cot, "core", 2, 1) for cot in second]
    *arrived, other_keep, kept, act_own = lax.optimization_barrier(
        (*first, *second, *others, *received, other_keep, kept, act_own)
    )
    first, second, others, received = arrived[:FIRST], arrived[FIRST:8], arrived[8:13], arrived[13:]
    act_recv = exchange(act_own, "core", 2, 1)
    summed = second_call(rows, second, others, keep, other_keep, kept, received)
    summed, act_recv = lax.optimization_barrier((summed, act_recv))
    summed = lax.psum_scatter(summed, "z", scatter_dimension=0, tiled=True)
    gradient, row_sums, col_sums = gradient_call(rows, halves, first + second, [act_own, act_recv])

    row_sums = total(reduce_four(row_sums, "x", 4, (1, 2, 3)), "yh", 2)
    row_stats = decay_rate * row_prev + (1.0 - decay_rate) * (row_sums / D)
    scaled = gradient * lax.rsqrt(row_stats)[:, None]
    sums = jnp.concatenate([col_sums, jnp.sum(scaled * scaled, axis=0), row_stats])
    sums = total(total(sums, "core", 2), "yl", 2)
    sums = sums + exchange(sums, "z", 8, 1)
    sums = reduce_four(sums, "z", 8, (2, 4, 6))
    row_mean = jnp.sum(sums[1536:]) / FF
    col_stats = decay_rate * col_prev + (1.0 - decay_rate) * (sums[:768] / FF)
    part = jnp.sum((sums[768:1536] / col_stats).reshape(6, 128), axis=0)
    others = [exchange(part, "x", 4, bit) for bit in (1, 2, 3)]
    part = part + others[0]
    part, summed = lax.optimization_barrier((part, summed))
    part = total(part + others[1] + others[2], "yh", 2)

    summed = summed.reshape(8, 32, HALF)
    low, high = summed[:, :, :192], summed[:, :, 192:]
    mine = jnp.where(yl == 0, low, high)
    theirs = jnp.where(yl == 0, high, low)
    mine = (mine + exchange(theirs, "yl", 2, 1)).astype(jnp.bfloat16)
    input_grad = mine.reshape(256, 192)
    part, input_grad = lax.optimization_barrier((part, input_grad))

    squares_total = jnp.sum(part) * row_mean
    root_mean = jnp.sqrt(squares_total / (FF * D))
    unclipped = gradient * lax.rsqrt(row_stats[:, None] * col_stats[None, :] / row_mean)
    update = unclipped / jnp.maximum(1.0, root_mean)
    return (input_grad, update)


def solution(mesh):
    fine = Mesh(mesh.devices.reshape(4, 2, 2, 2, 8), ("x", "yh", "yl", "core", "z"))
    row, col = ("x", "yh"), ("yl", "core")
    return jax.shard_map(
        body,
        mesh=fine,
        in_specs=(
            P(("z",) + row, col),
            P("z", row + col),
            P(col + ("z",), row),
            P(col + ("z",)),
            P(row),
        ),
        out_specs=(P("z", row + col), P(col + ("z",), row)),
        check_vma=False,
    )
```

```python
import jax
import jax.numpy as jnp
from jax import lax
from jax.experimental.layout import Layout, with_layout_constraint
from jax.experimental import pallas as pl
from jax.experimental.pallas import tpu as pltpu
from jax.sharding import Mesh
from jax.sharding import PartitionSpec as P

D = 6144
FF = 24576
HALF = 384
FIRST, SECOND = 3, 5
VMEM = 28 * 1024 * 1024
ORDER = 16
STEP = 4

epsilon = 1e-30
decay_rate = 0.9


def exchange(value, axis, size, bit):
    return lax.ppermute(value, axis, [(i, i ^ bit) for i in range(size)])


def shift(value, axis, size, step):
    return lax.ppermute(value, axis, [(i, (i + step) % size) for i in range(size)])


def total(value, axis, size):
    bit = 1
    while bit < size:
        value = value + exchange(value, axis, size, bit)
        bit *= 2
    return value


def reduce_four(value, axis, size, bits):
    others = [exchange(value, axis, size, bit) for bit in bits]
    for other in others:
        value = value + other
    return value


def weight_kernel(core_ref, weight_ref, keep_ref, send_ref):
    weight = weight_ref[...]
    even = jnp.concatenate([weight[:, :192], weight[:, HALF : HALF + 192]], axis=1)
    odd = jnp.concatenate([weight[:, 192:HALF], weight[:, HALF + 192 :]], axis=1)
    first = core_ref[0] == 0
    keep_ref[...] = jnp.where(first, even, odd)
    send_ref[...] = jnp.where(first, odd, even)


def weight_call(halves, weight):
    spec = pl.BlockSpec((256, HALF), lambda s, halves: (s, 0))
    return pl.pallas_call(
        weight_kernel,
        grid_spec=pltpu.PrefetchScalarGridSpec(
            num_scalar_prefetch=1,
            grid=(3,),
            in_specs=[pl.BlockSpec((256, 768), lambda s, halves: (s, 0))],
            out_specs=[spec, spec],
        ),
        out_shape=[jax.ShapeDtypeStruct((768, HALF), jnp.bfloat16)] * 2,
        compiler_params=pltpu.CompilerParams(vmem_limit_bytes=VMEM),
    )(halves, weight)


VECTORS = pl.BlockSpec(memory_space=pltpu.VMEM)
SCALARS = pl.BlockSpec(memory_space=pltpu.SMEM)
PARAMS = pltpu.CompilerParams(vmem_limit_bytes=60 * 1024 * 1024)


def tokens(refs):
    return jnp.concatenate([ref[...].reshape(-1, 768) for ref in refs], axis=0)


def first_kernel(*refs):
    cot = tokens(refs[:FIRST])
    keep_ref, send_ref, out, *sent = refs[FIRST:]
    kept = jnp.dot(cot, keep_ref[...], preferred_element_type=jnp.float32)
    other = jnp.dot(cot, send_ref[...], preferred_element_type=jnp.float32)
    for j in range(FIRST):
        out[:, j] = kept[j * 256 : (j + 1) * 256].reshape(8, 32, HALF)
        sent[j][...] = other[j * 256 : (j + 1) * 256].reshape(8, 32, HALF)


def second_kernel(rows_ref, *refs):
    cots, others = tokens(refs[:SECOND]), tokens(refs[SECOND : 2 * SECOND])
    keep_ref, other_ref, before_ref, *received, out = refs[2 * SECOND :]
    part = jnp.dot(cots, keep_ref[...], preferred_element_type=jnp.float32) + jnp.dot(
        others, other_ref[...], preferred_element_type=jnp.float32
    )
    for j in range(FIRST):
        out[:, rows_ref[j]] = before_ref[:, j] + received[j][...]
    for j in range(SECOND):
        rows = part[j * STEP * 32 : (j + 1) * STEP * 32]
        out[:, rows_ref[FIRST + j]] = rows.reshape(STEP, 32, HALF)


def first_call(cots, keep, send):
    return pl.pallas_call(
        first_kernel,
        in_specs=[VECTORS] * (FIRST + 2),
        out_specs=[VECTORS] * (1 + FIRST),
        out_shape=[jax.ShapeDtypeStruct((8, FIRST, 32, HALF), jnp.float32)]
        + [jax.ShapeDtypeStruct((8, 32, HALF), jnp.float32)] * FIRST,
        compiler_params=PARAMS,
        cost_estimate=pl.CostEstimate(
            flops=ORDER * FIRST * 4 * 256 * 768 * HALF, bytes_accessed=ORDER * 4 * 1024 * 1024, transcendentals=0
        ),
    )(*cots, keep, send)


def second_call(rows, cots, others, keep, other_keep, before, received):
    def step_spec(*shape):
        return pl.BlockSpec((STEP, *shape), lambda s, rows: (s,) + (0,) * len(shape))

    weight = pl.BlockSpec((768, HALF), lambda s, rows: (0, 0))
    return pl.pallas_call(
        second_kernel,
        grid_spec=pltpu.PrefetchScalarGridSpec(
            num_scalar_prefetch=1,
            grid=(8 // STEP,),
            in_specs=[step_spec(32, 768)] * (2 * SECOND)
            + [weight] * 2
            + [step_spec(FIRST, 32, HALF)]
            + [step_spec(32, HALF)] * FIRST,
            out_specs=step_spec(8, 32, HALF),
        ),
        out_shape=jax.ShapeDtypeStruct((8, 8, 32, HALF), jnp.float32),
        compiler_params=pltpu.CompilerParams(vmem_limit_bytes=60 * 1024 * 1024),
        cost_estimate=pl.CostEstimate(
            flops=SECOND * 4 * 256 * 768 * HALF, bytes_accessed=8 * 1024 * 1024, transcendentals=0
        ),
    )(rows, *cots, *others, keep, other_keep, before, *received)


def gradient_kernel(rows_ref, halves_ref, *refs):
    cots, acts, (out_ref, row_ref, col_ref) = refs[:8], refs[8:10], refs[10:]
    act = jnp.concatenate(
        [
            jnp.concatenate([a[:, rows_ref[j]].reshape(256, HALF) for j in range(8)], axis=0)
            for a in acts
        ],
        axis=1,
    )
    whole = lax.dot_general(
        tokens(cots), act, (((0,), (0,)), ((), ())), preferred_element_type=jnp.float32
    )
    for h in range(2):
        columns = pl.ds(pl.multiple_of(halves_ref[h] * HALF, HALF), HALF)
        out_ref[:, columns] = whole[:, h * HALF : (h + 1) * HALF]
    gradient = out_ref[...]
    square = gradient * gradient + epsilon
    col_ref[...] = jnp.sum(square, axis=0)
    lanes = sum(square[:, k * 128 : (k + 1) * 128] for k in range(6))
    row_ref[...] = jnp.sum(lanes.T, axis=0)


def gradient_call(rows, halves, cots, acts):
    return pl.pallas_call(
        gradient_kernel,
        in_specs=[SCALARS] * 2 + [VECTORS] * 10,
        out_specs=[VECTORS] * 3,
        out_shape=[
            jax.ShapeDtypeStruct((768, 768), jnp.float32),
            jax.ShapeDtypeStruct((768,), jnp.float32),
            jax.ShapeDtypeStruct((768,), jnp.float32),
        ],
        compiler_params=PARAMS,
        cost_estimate=pl.CostEstimate(
            flops=2 * 2048 * 768 * 768, bytes_accessed=9 * 1024 * 1024, transcendentals=0
        ),
    )(rows, halves, *cots, *acts)


def body(cotangent, activations, weight, row_prev, col_prev):
    x, yh, core = lax.axis_index("x"), lax.axis_index("yh"), lax.axis_index("core")
    yl = lax.axis_index("yl")

    near = lax.ppermute(activations, ("yl", "core"), [(0, 2), (3, 1), (1, 0), (2, 3)])
    cross = lax.ppermute(activations, ("yl", "core"), [(1, 2), (2, 1)])
    same = jnp.where(yl == core, activations, near)
    opposite = jnp.where(yl == core, near, cross)
    act_half = jnp.where(
        core == 0,
        jnp.concatenate([same, opposite], axis=1),
        jnp.concatenate([opposite, same], axis=1),
    )
    act_half = with_layout_constraint(act_half, Layout((0, 1)))
    blocks = cotangent.reshape(32, 8, 768).transpose(1, 0, 2)
    act_own = lax.all_gather(act_half, "z", axis=0, tiled=True)
    act_own = with_layout_constraint(act_own, Layout((0, 1))).reshape(8, 8, 32, HALF)

    own_cot = lax.all_to_all(blocks, "z", 0, 0, tiled=True)
    own_cot, weight, act_half = lax.optimization_barrier((own_cot, weight, act_half))
    right, left, far = (x + 3) % 4, (x + 1) % 4, (x + 2) % 4
    columns = [x, x, far, right, left, far, right, left]
    sides = [yh, 1 - yh, yh, yh, yh, 1 - yh, 1 - yh, 1 - yh]
    rows = jnp.stack([c * 2 + side for c, side in zip(columns, sides)]).astype(jnp.int32)
    halves = jnp.stack([core, 1 - core]).astype(jnp.int32)
    keep, send = weight_call(halves, weight)

    other_cot = exchange(own_cot, "yh", 2, 1)
    other_cot, keep, send, rows, halves = lax.optimization_barrier((other_cot, keep, send, rows, halves))
    right_cot = shift(own_cot, "x", 4, 1)
    left_cot = shift(own_cot, "x", 4, -1)
    far_cot = shift(own_cot, "x", 4, 2)
    other_right = shift(other_cot, "x", 4, 1)
    other_left = shift(other_cot, "x", 4, -1)
    other_far = exchange(far_cot, "yh", 2, 1)
    first = [own_cot, other_cot, far_cot]
    second = [right_cot, left_cot, other_far, other_right, other_left]

    kept, *sent = first_call(first, keep, send)
    second[0], second[1], second[2], send, *sent = lax.optimization_barrier(
        (second[0], second[1], second[2], send, *sent)
    )
    received = [exchange(part, "core", 2, 1) for part in sent]
    others = [exchange(cot, "core", 2, 1) for cot in second]
    other_keep = exchange(send, "core", 2, 1)
    *arrived, other_keep, kept, act_own = lax.optimization_barrier(
        (*first, *second, *others, *received, other_keep, kept, act_own)
    )
    first, second, others, received = arrived[:FIRST], arrived[FIRST:8], arrived[8:13], arrived[13:]
    act_recv = exchange(act_own, "core", 2, 1)
    summed = second_call(rows, second, others, keep, other_keep, kept, received)
    summed, act_recv = lax.optimization_barrier((summed, act_recv))
    summed = lax.psum_scatter(summed, "z", scatter_dimension=0, tiled=True)
    gradient, row_sums, col_sums = gradient_call(rows, halves, first + second, [act_own, act_recv])

    row_sums = total(reduce_four(row_sums, "x", 4, (1, 2, 3)), "yh", 2)
    row_stats = decay_rate * row_prev + (1.0 - decay_rate) * (row_sums / D)
    scaled = gradient * lax.rsqrt(row_stats)[:, None]
    sums = jnp.concatenate([col_sums, jnp.sum(scaled * scaled, axis=0), row_stats])
    sums = total(total(sums, "core", 2), "yl", 2)
    sums = sums + exchange(sums, "z", 8, 1)
    sums = reduce_four(sums, "z", 8, (2, 4, 6))
    row_mean = jnp.sum(sums[1536:]) / FF
    col_stats = decay_rate * col_prev + (1.0 - decay_rate) * (sums[:768] / FF)
    part = jnp.sum((sums[768:1536] / col_stats).reshape(6, 128), axis=0)
    others = [exchange(part, "x", 4, bit) for bit in (1, 2, 3)]
    part = part + others[0]
    part, summed = lax.optimization_barrier((part, summed))
    part = total(part + others[1] + others[2], "yh", 2)

    summed = summed.reshape(8, 32, HALF)
    low, high = summed[:, :, :192], summed[:, :, 192:]
    mine = jnp.where(yl == 0, low, high)
    theirs = jnp.where(yl == 0, high, low)
    mine = (mine + exchange(theirs, "yl", 2, 1)).astype(jnp.bfloat16)
    input_grad = mine.reshape(256, 192)
    part, input_grad = lax.optimization_barrier((part, input_grad))

    squares_total = jnp.sum(part) * row_mean
    root_mean = jnp.sqrt(squares_total / (FF * D))
    unclipped = gradient * lax.rsqrt(row_stats[:, None] * col_stats[None, :] / row_mean)
    update = unclipped / jnp.maximum(1.0, root_mean)
    return (input_grad, update)


def solution(mesh):
    fine = Mesh(mesh.devices.reshape(4, 2, 2, 2, 8), ("x", "yh", "yl", "core", "z"))
    row, col = ("x", "yh"), ("yl", "core")
    return jax.shard_map(
        body,
        mesh=fine,
        in_specs=(
            P(("z",) + row, col),
            P("z", row + col),
            P(col + ("z",), row),
            P(col + ("z",)),
            P(row),
        ),
        out_specs=(P("z", row + col), P(col + ("z",), row)),
        check_vma=False,
    )
```

```python
import jax
import jax.numpy as jnp
from jax import lax
from jax.experimental.layout import Layout, with_layout_constraint
from jax.experimental import pallas as pl
from jax.experimental.pallas import tpu as pltpu
from jax.sharding import Mesh
from jax.sharding import PartitionSpec as P

D = 6144
FF = 24576
HALF = 384
FIRST, SECOND = 3, 5
VMEM = 28 * 1024 * 1024
ORDER = 16
STEP = 4

epsilon = 1e-30
decay_rate = 0.9


def exchange(value, axis, size, bit):
    return lax.ppermute(value, axis, [(i, i ^ bit) for i in range(size)])


def shift(value, axis, size, step):
    return lax.ppermute(value, axis, [(i, (i + step) % size) for i in range(size)])


def total(value, axis, size):
    bit = 1
    while bit < size:
        value = value + exchange(value, axis, size, bit)
        bit *= 2
    return value


def reduce_four(value, axis, size, bits):
    others = [exchange(value, axis, size, bit) for bit in bits]
    for other in others:
        value = value + other
    return value


def weight_kernel(core_ref, weight_ref, keep_ref, send_ref):
    weight = weight_ref[...]
    even = jnp.concatenate([weight[:, :192], weight[:, HALF : HALF + 192]], axis=1)
    odd = jnp.concatenate([weight[:, 192:HALF], weight[:, HALF + 192 :]], axis=1)
    first = core_ref[0] == 0
    keep_ref[...] = jnp.where(first, even, odd)
    send_ref[...] = jnp.where(first, odd, even)


def weight_call(halves, weight):
    spec = pl.BlockSpec((256, HALF), lambda s, halves: (s, 0))
    return pl.pallas_call(
        weight_kernel,
        grid_spec=pltpu.PrefetchScalarGridSpec(
            num_scalar_prefetch=1,
            grid=(3,),
            in_specs=[pl.BlockSpec((256, 768), lambda s, halves: (s, 0))],
            out_specs=[spec, spec],
        ),
        out_shape=[jax.ShapeDtypeStruct((768, HALF), jnp.bfloat16)] * 2,
        compiler_params=pltpu.CompilerParams(vmem_limit_bytes=VMEM),
    )(halves, weight)


VECTORS = pl.BlockSpec(memory_space=pltpu.VMEM)
SCALARS = pl.BlockSpec(memory_space=pltpu.SMEM)
PARAMS = pltpu.CompilerParams(vmem_limit_bytes=60 * 1024 * 1024)


def tokens(refs):
    return jnp.concatenate([ref[...].reshape(-1, 768) for ref in refs], axis=0)


def first_kernel(*refs):
    cot = tokens(refs[:FIRST])
    keep_ref, send_ref, out, *sent = refs[FIRST:]
    kept = jnp.dot(cot, keep_ref[...], preferred_element_type=jnp.float32)
    other = jnp.dot(cot, send_ref[...], preferred_element_type=jnp.float32)
    for j in range(FIRST):
        out[:, j] = kept[j * 256 : (j + 1) * 256].reshape(8, 32, HALF)
        sent[j][...] = other[j * 256 : (j + 1) * 256].reshape(8, 32, HALF)


def second_kernel(rows_ref, *refs):
    cots, others = tokens(refs[:SECOND]), tokens(refs[SECOND : 2 * SECOND])
    keep_ref, other_ref, before_ref, *received, out = refs[2 * SECOND :]
    part = jnp.dot(cots, keep_ref[...], preferred_element_type=jnp.float32) + jnp.dot(
        others, other_ref[...], preferred_element_type=jnp.float32
    )
    for j in range(FIRST):
        out[:, rows_ref[j]] = before_ref[:, j] + received[j][...]
    for j in range(SECOND):
        rows = part[j * STEP * 32 : (j + 1) * STEP * 32]
        out[:, rows_ref[FIRST + j]] = rows.reshape(STEP, 32, HALF)


def first_call(cots, keep, send):
    return pl.pallas_call(
        first_kernel,
        in_specs=[VECTORS] * (FIRST + 2),
        out_specs=[VECTORS] * (1 + FIRST),
        out_shape=[jax.ShapeDtypeStruct((8, FIRST, 32, HALF), jnp.float32)]
        + [jax.ShapeDtypeStruct((8, 32, HALF), jnp.float32)] * FIRST,
        compiler_params=PARAMS,
        cost_estimate=pl.CostEstimate(
            flops=ORDER * FIRST * 4 * 256 * 768 * HALF, bytes_accessed=ORDER * 4 * 1024 * 1024, transcendentals=0
        ),
    )(*cots, keep, send)


def second_call(rows, cots, others, keep, other_keep, before, received):
    def step_spec(*shape):
        return pl.BlockSpec((STEP, *shape), lambda s, rows: (s,) + (0,) * len(shape))

    weight = pl.BlockSpec((768, HALF), lambda s, rows: (0, 0))
    return pl.pallas_call(
        second_kernel,
        grid_spec=pltpu.PrefetchScalarGridSpec(
            num_scalar_prefetch=1,
            grid=(8 // STEP,),
            in_specs=[step_spec(32, 768)] * (2 * SECOND)
            + [weight] * 2
            + [step_spec(FIRST, 32, HALF)]
            + [step_spec(32, HALF)] * FIRST,
            out_specs=step_spec(8, 32, HALF),
        ),
        out_shape=jax.ShapeDtypeStruct((8, 8, 32, HALF), jnp.float32),
        compiler_params=pltpu.CompilerParams(vmem_limit_bytes=50 * 1024 * 1024),
        cost_estimate=pl.CostEstimate(
            flops=SECOND * 4 * 256 * 768 * HALF, bytes_accessed=8 * 1024 * 1024, transcendentals=0
        ),
    )(rows, *cots, *others, keep, other_keep, before, *received)


def gradient_kernel(rows_ref, halves_ref, *refs):
    cots, acts, (out_ref, row_ref, col_ref) = refs[:8], refs[8:10], refs[10:]
    act = jnp.concatenate(
        [
            jnp.concatenate([a[:, rows_ref[j]].reshape(256, HALF) for j in range(8)], axis=0)
            for a in acts
        ],
        axis=1,
    )
    whole = lax.dot_general(
        tokens(cots), act, (((0,), (0,)), ((), ())), preferred_element_type=jnp.float32
    )
    for h in range(2):
        columns = pl.ds(pl.multiple_of(halves_ref[h] * HALF, HALF), HALF)
        out_ref[:, columns] = whole[:, h * HALF : (h + 1) * HALF]
    gradient = out_ref[...]
    square = gradient * gradient + epsilon
    col_ref[...] = jnp.sum(square, axis=0)
    lanes = sum(square[:, k * 128 : (k + 1) * 128] for k in range(6))
    row_ref[...] = jnp.sum(lanes.T, axis=0)


def gradient_call(rows, halves, cots, acts):
    return pl.pallas_call(
        gradient_kernel,
        in_specs=[SCALARS] * 2 + [VECTORS] * 10,
        out_specs=[VECTORS] * 3,
        out_shape=[
            jax.ShapeDtypeStruct((768, 768), jnp.float32),
            jax.ShapeDtypeStruct((768,), jnp.float32),
            jax.ShapeDtypeStruct((768,), jnp.float32),
        ],
        compiler_params=PARAMS,
        cost_estimate=pl.CostEstimate(
            flops=2 * 2048 * 768 * 768, bytes_accessed=9 * 1024 * 1024, transcendentals=0
        ),
    )(rows, halves, *cots, *acts)


def body(cotangent, activations, weight, row_prev, col_prev):
    x, yh, core = lax.axis_index("x"), lax.axis_index("yh"), lax.axis_index("core")
    yl = lax.axis_index("yl")

    near = lax.ppermute(activations, ("yl", "core"), [(0, 2), (3, 1), (1, 0), (2, 3)])
    cross = lax.ppermute(activations, ("yl", "core"), [(1, 2), (2, 1)])
    same = jnp.where(yl == core, activations, near)
    opposite = jnp.where(yl == core, near, cross)
    act_half = jnp.where(
        core == 0,
        jnp.concatenate([same, opposite], axis=1),
        jnp.concatenate([opposite, same], axis=1),
    )
    act_half = with_layout_constraint(act_half, Layout((0, 1)))
    blocks = cotangent.reshape(32, 8, 768).transpose(1, 0, 2)
    act_own = lax.all_gather(act_half, "z", axis=0, tiled=True)
    act_own = with_layout_constraint(act_own, Layout((0, 1))).reshape(8, 8, 32, HALF)

    own_cot = lax.all_to_all(blocks, "z", 0, 0, tiled=True)
    own_cot, weight, act_half = lax.optimization_barrier((own_cot, weight, act_half))
    right, left, far = (x + 3) % 4, (x + 1) % 4, (x + 2) % 4
    columns = [x, x, far, right, left, far, right, left]
    sides = [yh, 1 - yh, yh, yh, yh, 1 - yh, 1 - yh, 1 - yh]
    rows = jnp.stack([c * 2 + side for c, side in zip(columns, sides)]).astype(jnp.int32)
    halves = jnp.stack([core, 1 - core]).astype(jnp.int32)
    keep, send = weight_call(halves, weight)

    other_cot = exchange(own_cot, "yh", 2, 1)
    other_cot, keep, send, rows, halves = lax.optimization_barrier((other_cot, keep, send, rows, halves))
    right_cot = shift(own_cot, "x", 4, 1)
    left_cot = shift(own_cot, "x", 4, -1)
    far_cot = shift(own_cot, "x", 4, 2)
    other_right = shift(other_cot, "x", 4, 1)
    other_left = shift(other_cot, "x", 4, -1)
    other_far = exchange(far_cot, "yh", 2, 1)
    first = [own_cot, other_cot, far_cot]
    second = [right_cot, left_cot, other_far, other_right, other_left]

    kept, *sent = first_call(first, keep, send)
    second[0], second[1], second[2], send, *sent = lax.optimization_barrier(
        (second[0], second[1], second[2], send, *sent)
    )
    received = [exchange(part, "core", 2, 1) for part in sent]
    others = [exchange(cot, "core", 2, 1) for cot in second]
    other_keep = exchange(send, "core", 2, 1)
    *arrived, other_keep, kept, act_own = lax.optimization_barrier(
        (*first, *second, *others, *received, other_keep, kept, act_own)
    )
    first, second, others, received = arrived[:FIRST], arrived[FIRST:8], arrived[8:13], arrived[13:]
    act_recv = exchange(act_own, "core", 2, 1)
    summed = second_call(rows, second, others, keep, other_keep, kept, received)
    summed, act_recv = lax.optimization_barrier((summed, act_recv))
    summed = lax.psum_scatter(summed, "z", scatter_dimension=0, tiled=True)
    gradient, row_sums, col_sums = gradient_call(rows, halves, first + second, [act_own, act_recv])

    row_sums = total(reduce_four(row_sums, "x", 4, (1, 2, 3)), "yh", 2)
    row_stats = decay_rate * row_prev + (1.0 - decay_rate) * (row_sums / D)
    scaled = gradient * lax.rsqrt(row_stats)[:, None]
    sums = jnp.concatenate([col_sums, jnp.sum(scaled * scaled, axis=0), row_stats])
    sums = total(total(sums, "core", 2), "yl", 2)
    sums = sums + exchange(sums, "z", 8, 1)
    sums = reduce_four(sums, "z", 8, (2, 4, 6))
    row_mean = jnp.sum(sums[1536:]) / FF
    col_stats = decay_rate * col_prev + (1.0 - decay_rate) * (sums[:768] / FF)
    part = jnp.sum((sums[768:1536] / col_stats).reshape(6, 128), axis=0)
    others = [exchange(part, "x", 4, bit) for bit in (1, 2, 3)]
    part = part + others[0]
    part, summed = lax.optimization_barrier((part, summed))
    part = total(part + others[1] + others[2], "yh", 2)

    summed = summed.reshape(8, 32, HALF)
    low, high = summed[:, :, :192], summed[:, :, 192:]
    mine = jnp.where(yl == 0, low, high)
    theirs = jnp.where(yl == 0, high, low)
    mine = (mine + exchange(theirs, "yl", 2, 1)).astype(jnp.bfloat16)
    input_grad = mine.reshape(256, 192)
    part, input_grad = lax.optimization_barrier((part, input_grad))

    squares_total = jnp.sum(part) * row_mean
    root_mean = jnp.sqrt(squares_total / (FF * D))
    unclipped = gradient * lax.rsqrt(row_stats[:, None] * col_stats[None, :] / row_mean)
    update = unclipped / jnp.maximum(1.0, root_mean)
    return (input_grad, update)


def solution(mesh):
    fine = Mesh(mesh.devices.reshape(4, 2, 2, 2, 8), ("x", "yh", "yl", "core", "z"))
    row, col = ("x", "yh"), ("yl", "core")
    return jax.shard_map(
        body,
        mesh=fine,
        in_specs=(
            P(("z",) + row, col),
            P("z", row + col),
            P(col + ("z",), row),
            P(col + ("z",)),
            P(row),
        ),
        out_specs=(P("z", row + col), P(col + ("z",), row)),
        check_vma=False,
    )
```

```python
import jax
import jax.numpy as jnp
from jax import lax
from jax.experimental.layout import Layout, with_layout_constraint
from jax.experimental import pallas as pl
from jax.experimental.pallas import tpu as pltpu
from jax.sharding import Mesh
from jax.sharding import PartitionSpec as P

D = 6144
FF = 24576
HALF = 384
FIRST, SECOND = 3, 5
VMEM = 28 * 1024 * 1024
ORDER = 16
STEP = 4

epsilon = 1e-30
decay_rate = 0.9


def exchange(value, axis, size, bit):
    return lax.ppermute(value, axis, [(i, i ^ bit) for i in range(size)])


def shift(value, axis, size, step):
    return lax.ppermute(value, axis, [(i, (i + step) % size) for i in range(size)])


def total(value, axis, size):
    bit = 1
    while bit < size:
        value = value + exchange(value, axis, size, bit)
        bit *= 2
    return value


def reduce_four(value, axis, size, bits):
    others = [exchange(value, axis, size, bit) for bit in bits]
    for other in others:
        value = value + other
    return value


def weight_kernel(core_ref, weight_ref, keep_ref, send_ref):
    weight = weight_ref[...]
    even = jnp.concatenate([weight[:, :192], weight[:, HALF : HALF + 192]], axis=1)
    odd = jnp.concatenate([weight[:, 192:HALF], weight[:, HALF + 192 :]], axis=1)
    first = core_ref[0] == 0
    keep_ref[...] = jnp.where(first, even, odd)
    send_ref[...] = jnp.where(first, odd, even)


def weight_call(halves, weight):
    spec = pl.BlockSpec((256, HALF), lambda s, halves: (s, 0))
    return pl.pallas_call(
        weight_kernel,
        grid_spec=pltpu.PrefetchScalarGridSpec(
            num_scalar_prefetch=1,
            grid=(3,),
            in_specs=[pl.BlockSpec((256, 768), lambda s, halves: (s, 0))],
            out_specs=[spec, spec],
        ),
        out_shape=[jax.ShapeDtypeStruct((768, HALF), jnp.bfloat16)] * 2,
        compiler_params=pltpu.CompilerParams(vmem_limit_bytes=VMEM),
    )(halves, weight)


VECTORS = pl.BlockSpec(memory_space=pltpu.VMEM)
SCALARS = pl.BlockSpec(memory_space=pltpu.SMEM)
PARAMS = pltpu.CompilerParams(vmem_limit_bytes=60 * 1024 * 1024)


def tokens(refs):
    return jnp.concatenate([ref[...].reshape(-1, 768) for ref in refs], axis=0)


def first_kernel(*refs):
    cot = tokens(refs[:FIRST])
    keep_ref, send_ref, out, *sent = refs[FIRST:]
    kept = jnp.dot(cot, keep_ref[...], preferred_element_type=jnp.float32)
    other = jnp.dot(cot, send_ref[...], preferred_element_type=jnp.float32)
    for j in range(FIRST):
        out[:, j] = kept[j * 256 : (j + 1) * 256].reshape(8, 32, HALF)
        sent[j][...] = other[j * 256 : (j + 1) * 256].reshape(8, 32, HALF)


def second_kernel(rows_ref, *refs):
    cots, others = tokens(refs[:SECOND]), tokens(refs[SECOND : 2 * SECOND])
    keep_ref, other_ref, before_ref, *received, out = refs[2 * SECOND :]
    part = jnp.dot(cots, keep_ref[...], preferred_element_type=jnp.float32) + jnp.dot(
        others, other_ref[...], preferred_element_type=jnp.float32
    )
    for j in range(FIRST):
        out[:, rows_ref[j]] = before_ref[:, j] + received[j][...]
    for j in range(SECOND):
        rows = part[j * STEP * 32 : (j + 1) * STEP * 32]
        out[:, rows_ref[FIRST + j]] = rows.reshape(STEP, 32, HALF)


def first_call(cots, keep, send):
    return pl.pallas_call(
        first_kernel,
        in_specs=[VECTORS] * (FIRST + 2),
        out_specs=[VECTORS] * (1 + FIRST),
        out_shape=[jax.ShapeDtypeStruct((8, FIRST, 32, HALF), jnp.float32)]
        + [jax.ShapeDtypeStruct((8, 32, HALF), jnp.float32)] * FIRST,
        compiler_params=PARAMS,
        cost_estimate=pl.CostEstimate(
            flops=ORDER * FIRST * 4 * 256 * 768 * HALF, bytes_accessed=ORDER * 4 * 1024 * 1024, transcendentals=0
        ),
    )(*cots, keep, send)


def second_call(rows, cots, others, keep, other_keep, before, received):
    def step_spec(*shape):
        return pl.BlockSpec((STEP, *shape), lambda s, rows: (s,) + (0,) * len(shape))

    weight = pl.BlockSpec((768, HALF), lambda s, rows: (0, 0))
    return pl.pallas_call(
        second_kernel,
        grid_spec=pltpu.PrefetchScalarGridSpec(
            num_scalar_prefetch=1,
            grid=(8 // STEP,),
            in_specs=[step_spec(32, 768)] * (2 * SECOND)
            + [weight] * 2
            + [step_spec(FIRST, 32, HALF)]
            + [step_spec(32, HALF)] * FIRST,
            out_specs=step_spec(8, 32, HALF),
        ),
        out_shape=jax.ShapeDtypeStruct((8, 8, 32, HALF), jnp.float32),
        compiler_params=pltpu.CompilerParams(vmem_limit_bytes=60 * 1024 * 1024),
        cost_estimate=pl.CostEstimate(
            flops=SECOND * 4 * 256 * 768 * HALF, bytes_accessed=8 * 1024 * 1024, transcendentals=0
        ),
    )(rows, *cots, *others, keep, other_keep, before, *received)


def gradient_kernel(rows_ref, halves_ref, *refs):
    cots, acts, (out_ref, row_ref, col_ref) = refs[:8], refs[8:10], refs[10:]
    act = jnp.concatenate(
        [
            jnp.concatenate([a[:, rows_ref[j]].reshape(256, HALF) for j in range(8)], axis=0)
            for a in acts
        ],
        axis=1,
    )
    whole = lax.dot_general(
        tokens(cots), act, (((0,), (0,)), ((), ())), preferred_element_type=jnp.float32
    )
    for h in range(2):
        columns = pl.ds(pl.multiple_of(halves_ref[h] * HALF, HALF), HALF)
        out_ref[:, columns] = whole[:, h * HALF : (h + 1) * HALF]
    gradient = out_ref[...]
    square = gradient * gradient + epsilon
    col_ref[...] = jnp.sum(square, axis=0)
    lanes = sum(square[:, k * 128 : (k + 1) * 128] for k in range(6))
    row_ref[...] = jnp.sum(lanes.T, axis=0)


def gradient_call(rows, halves, cots, acts):
    return pl.pallas_call(
        gradient_kernel,
        in_specs=[SCALARS] * 2 + [VECTORS] * 10,
        out_specs=[VECTORS] * 3,
        out_shape=[
            jax.ShapeDtypeStruct((768, 768), jnp.float32),
            jax.ShapeDtypeStruct((768,), jnp.float32),
            jax.ShapeDtypeStruct((768,), jnp.float32),
        ],
        compiler_params=PARAMS,
        cost_estimate=pl.CostEstimate(
            flops=2 * 2048 * 768 * 768, bytes_accessed=9 * 1024 * 1024, transcendentals=0
        ),
    )(rows, halves, *cots, *acts)


def body(cotangent, activations, weight, row_prev, col_prev):
    x, yh, core = lax.axis_index("x"), lax.axis_index("yh"), lax.axis_index("core")
    yl = lax.axis_index("yl")

    near = lax.ppermute(activations, ("yl", "core"), [(0, 2), (3, 1), (1, 0), (2, 3)])
    cross = lax.ppermute(activations, ("yl", "core"), [(1, 2), (2, 1)])
    same = jnp.where(yl == core, activations, near)
    opposite = jnp.where(yl == core, near, cross)
    act_half = jnp.where(
        core == 0,
        jnp.concatenate([same, opposite], axis=1),
        jnp.concatenate([opposite, same], axis=1),
    )
    act_half = with_layout_constraint(act_half, Layout((0, 1)))
    blocks = cotangent.reshape(32, 8, 768).transpose(1, 0, 2)
    act_own = lax.all_gather(act_half, "z", axis=0, tiled=True)
    act_own = with_layout_constraint(act_own, Layout((0, 1))).reshape(8, 8, 32, HALF)

    own_cot = lax.all_to_all(blocks, "z", 0, 0, tiled=True)
    act_half, weight = lax.optimization_barrier((act_half, weight))
    own_cot, act_half = lax.optimization_barrier((own_cot, act_half))
    right, left, far = (x + 3) % 4, (x + 1) % 4, (x + 2) % 4
    columns = [x, x, far, right, left, far, right, left]
    sides = [yh, 1 - yh, yh, yh, yh, 1 - yh, 1 - yh, 1 - yh]
    rows = jnp.stack([c * 2 + side for c, side in zip(columns, sides)]).astype(jnp.int32)
    halves = jnp.stack([core, 1 - core]).astype(jnp.int32)
    keep, send = weight_call(halves, weight)

    other_cot = exchange(own_cot, "yh", 2, 1)
    other_keep = exchange(send, "core", 2, 1)
    other_cot, keep, send, other_keep, rows, halves = lax.optimization_barrier(
        (other_cot, keep, send, other_keep, rows, halves)
    )
    right_cot = shift(own_cot, "x", 4, 1)
    left_cot = shift(own_cot, "x", 4, -1)
    far_cot = shift(own_cot, "x", 4, 2)
    other_right = shift(other_cot, "x", 4, 1)
    other_left = shift(other_cot, "x", 4, -1)
    other_far = exchange(far_cot, "yh", 2, 1)
    first = [own_cot, other_cot, far_cot]
    second = [right_cot, left_cot, other_far, other_right, other_left]

    kept, *sent = first_call(first, keep, send)
    second[0], second[1], second[2], *sent = lax.optimization_barrier(
        (second[0], second[1], second[2], *sent)
    )
    received = [exchange(part, "core", 2, 1) for part in sent]
    others = [exchange(cot, "core", 2, 1) for cot in second]
    *arrived, kept, act_own = lax.optimization_barrier(
        (*first, *second, *others, *received, kept, act_own)
    )
    first, second, others, received = arrived[:FIRST], arrived[FIRST:8], arrived[8:13], arrived[13:]
    act_recv = exchange(act_own, "core", 2, 1)
    summed = second_call(rows, second, others, keep, other_keep, kept, received)
    summed, act_recv = lax.optimization_barrier((summed, act_recv))
    summed = lax.psum_scatter(summed, "z", scatter_dimension=0, tiled=True)
    gradient, row_sums, col_sums = gradient_call(rows, halves, first + second, [act_own, act_recv])

    row_sums = total(reduce_four(row_sums, "x", 4, (1, 2, 3)), "yh", 2)
    row_stats = decay_rate * row_prev + (1.0 - decay_rate) * (row_sums / D)
    scaled = gradient * lax.rsqrt(row_stats)[:, None]
    sums = jnp.concatenate([col_sums, jnp.sum(scaled * scaled, axis=0), row_stats])
    sums = total(total(sums, "core", 2), "yl", 2)
    sums = sums + exchange(sums, "z", 8, 1)
    sums = reduce_four(sums, "z", 8, (2, 4, 6))
    row_mean = jnp.sum(sums[1536:]) / FF
    col_stats = decay_rate * col_prev + (1.0 - decay_rate) * (sums[:768] / FF)
    part = jnp.sum((sums[768:1536] / col_stats).reshape(6, 128), axis=0)
    others = [exchange(part, "x", 4, bit) for bit in (1, 2, 3)]
    part = part + others[0]
    part, summed = lax.optimization_barrier((part, summed))
    part = total(part + others[1] + others[2], "yh", 2)

    summed = summed.reshape(8, 32, HALF)
    low, high = summed[:, :, :192], summed[:, :, 192:]
    mine = jnp.where(yl == 0, low, high)
    theirs = jnp.where(yl == 0, high, low)
    mine = (mine + exchange(theirs, "yl", 2, 1)).astype(jnp.bfloat16)
    input_grad = mine.reshape(256, 192)
    part, input_grad = lax.optimization_barrier((part, input_grad))

    squares_total = jnp.sum(part) * row_mean
    root_mean = jnp.sqrt(squares_total / (FF * D))
    unclipped = gradient * lax.rsqrt(row_stats[:, None] * col_stats[None, :] / row_mean)
    update = unclipped / jnp.maximum(1.0, root_mean)
    return (input_grad, update)


def solution(mesh):
    fine = Mesh(mesh.devices.reshape(4, 2, 2, 2, 8), ("x", "yh", "yl", "core", "z"))
    row, col = ("x", "yh"), ("yl", "core")
    return jax.shard_map(
        body,
        mesh=fine,
        in_specs=(
            P(("z",) + row, col),
            P("z", row + col),
            P(col + ("z",), row),
            P(col + ("z",)),
            P(row),
        ),
        out_specs=(P("z", row + col), P(col + ("z",), row)),
        check_vma=False,
    )
```
